512 devices in a mesh: tm: 32 (over z, x), height: 16 (over y, core).
Axes of the slice: x: 4, y: 8, z: 8, core: 2. Of those that a mesh axis runs over, the one named last changes fastest.
Arguments:
- video_latents: bfloat16 [64, 16, 160, 1024], P('tm', 'height'), may hold values from -6 to 6
- qkv_weight: bfloat16 [1024, 3072], P('tm'), may hold values from -0.1875 to 0.1875
- beta_weight: bfloat16 [1024, 8], replicated, may hold values from -0.1875 to 0.1875
- conv_kernel: float32 [3, 3, 3072], replicated, may hold values from -1.75 to 1.75
- decay_rate: float32 [64, 8], P('tm'), may hold values from 0 to 4, as said below
- step_rate: float32 [8], replicated, may hold values from 0.3 to 1.5
- output_gain: float32 [1024], replicated, may hold values from 0.25 to 1.75
Outputs:
- attended: bfloat16 [64, 16, 160, 1024], P('tm', 'height')
The draws below stay inside these ranges and needn't reach their ends.
Inputs may be any that keep to these rules, and one draw needn't show every extreme that they name: `decay_rate`: positive decay exponents.
All inputs are finite; a program needn't handle non-finite values.
Results may differ from the reference program's by a relative error of at most 0.008.
Values may be sent and summed in bfloat16 or wider, within the bound.
A program may use at most 128 MiB of HBM per device.

```python
import math
import jax
import jax.numpy as jnp
from jax import lax

HEADS = 8
DK = 128
D = 1024
COLS = 160
ROWS = 16
LATENT_FRAMES = 64


def draw_decay_rate(key, part):
    key = jax.random.fold_in(key, 7)
    random_subkeys = jax.random.split(key, 6)
    fast_share = 0.5
    is_fast = jax.random.uniform(random_subkeys[0], (HEADS,)) < fast_share
    fast_decay = jnp.exp(jax.random.uniform(random_subkeys[1], (HEADS,), minval=math.log(0.7), maxval=math.log(2.0)))
    slow_decay = jax.random.uniform(random_subkeys[2], (HEADS,), minval=0.1, maxval=0.5) / LATENT_FRAMES
    baseline_decay = jnp.where(is_fast, fast_decay, slow_decay)
    random_offset = jnp.exp(jax.random.uniform(random_subkeys[3], (LATENT_FRAMES, HEADS), minval=math.log(0.6), maxval=math.log(1.6)))
    cluster_frames = jax.random.randint(random_subkeys[4], (2,), 0, LATENT_FRAMES)
    cluster_lengths = jax.random.uniform(random_subkeys[5], (2,), minval=0.22, maxval=0.4)
    frame_cluster = jnp.sum((jnp.arange(LATENT_FRAMES)[:, None] == cluster_frames[None, :]) * cluster_lengths[None, :], axis=1)
    return (baseline_decay[None, :] * random_offset + frame_cluster[:, None]).astype(jnp.float32)


def level_of(own_key, extent, pieces, least, high):
    def one(position, parts):
        draws = jax.random.uniform(jax.random.fold_in(jax.random.fold_in(own_key, 6), position), (parts,), jnp.float32, least / len(pieces), high / len(pieces))
        return jnp.repeat(jnp.exp(draws), extent[position] // parts).reshape((-1,) + (1,) * (len(extent) - position - 1))

    level = one(*pieces[0])
    for cut in pieces[1:]:
        level = level * one(*cut)
    return level


def bell_draw(own_key, shape, width, bound, cuts=(), kind=jnp.bfloat16):
    array = width * jax.random.normal(own_key, shape, jnp.float32)
    if cuts:
        array = array * level_of(own_key, shape, cuts, -0.22, 0.18)
    return jnp.clip(array, -bound, bound).astype(kind)


def setup_inputs(seed: int = 0) -> dict:
    key_list = jax.random.split(jax.random.key(seed), 8)
    video_latents = bell_draw(key_list[0], (LATENT_FRAMES, ROWS, COLS, D), 1.0, 6.0, ((0, 32), (1, 16)))
    qkv_weight = bell_draw(key_list[1], (D, 3 * D), D ** -0.5, 0.1875, ((0, 32),))
    beta_weight = bell_draw(key_list[2], (D, HEADS), D ** -0.5, 0.1875)
    conv_kernel = bell_draw(key_list[3], (3, 3, 3 * D), 0.3, 1.75, (), jnp.float32)
    decay_rate = draw_decay_rate(jax.random.fold_in(key_list[7], 71), 0)
    step_rate = jnp.clip(jnp.exp(jax.random.uniform(key_list[5], (HEADS,), jnp.float32, math.log(0.3), math.log(1.5))), 0.3, 1.5)
    output_gain = jnp.clip(1.0 + 0.15 * jax.random.normal(key_list[6], (D,), jnp.float32), 0.25, 1.75)
    return {"video_latents": video_latents, "qkv_weight": qkv_weight, "beta_weight": beta_weight, "conv_kernel": conv_kernel, "decay_rate": decay_rate, "step_rate": step_rate, "output_gain": output_gain}


epsilon = 1e-06

def mix_stream(extended, kernel):
    count_rows = extended.shape[0] - 2
    count_cols = extended.shape[1]
    padded = jnp.pad(extended.astype(jnp.float32), ((0, 0), (1, 1), (0, 0)))
    summed = jnp.zeros((count_rows, count_cols, extended.shape[2]), jnp.float32)
    for offset_row in range(3):
        for offset_col in range(3):
            summed = summed + padded[offset_row:offset_row + count_rows, offset_col:offset_col + count_cols] * kernel[offset_row, offset_col]
    return jax.nn.silu(summed)

def normalize(entries):
    return entries * lax.rsqrt(lax.optimization_barrier(jnp.sum(entries * entries, axis=-1, keepdims=True)) + epsilon)

def advance(key_gram, written, decay_row, step_size):
    order_size = key_gram.shape[-1]
    identity = jnp.broadcast_to(jnp.eye(order_size, dtype=jnp.float32), key_gram.shape)
    system = identity + step_size[:, None, None] * key_gram
    factor = jnp.linalg.cholesky(system)
    stacked = jnp.concatenate([identity, step_size[:, None, None] * written], axis=2)
    halfway = lax.linalg.triangular_solve(factor, stacked, left_side=True, lower=True)
    solved = lax.linalg.triangular_solve(factor, halfway, left_side=True, lower=True, transpose_a=True)
    retain = jnp.exp(-decay_row)[:, None, None]
    return (retain * solved[:, :, :order_size], retain * solved[:, :, order_size:])

def reference(video_latents, qkv_weight, beta_weight, conv_kernel, decay_rate, step_rate, output_gain):
    model_width = HEADS * DK
    step_size = step_rate * (DK / (ROWS * COLS * LATENT_FRAMES))

    def per_frame(latents):
        flattened = latents.reshape(-1, model_width)
        projected = jnp.dot(flattened.astype(jnp.float32), qkv_weight.astype(jnp.float32), preferred_element_type=jnp.float32).astype(jnp.bfloat16)
        projected = lax.optimization_barrier(projected).reshape(ROWS, COLS, 3 * model_width)
        extended = jnp.pad(projected, ((1, 1), (0, 0), (0, 0)))
        streams = [mix_stream(extended[:, :, stream * model_width:(stream + 1) * model_width], conv_kernel[:, :, stream * model_width:(stream + 1) * model_width]).reshape(-1, HEADS, DK) for stream in range(3)]
        queries = normalize(streams[0]).astype(jnp.bfloat16)
        keys_unit = normalize(streams[1]).astype(jnp.bfloat16)
        values_b = streams[2].astype(jnp.bfloat16)
        beta_gates = jax.nn.sigmoid(jnp.dot(flattened.astype(jnp.float32), beta_weight.astype(jnp.float32), preferred_element_type=jnp.float32))
        queries, keys_unit, values_b = lax.optimization_barrier((queries, keys_unit, values_b))
        weighted = (beta_gates[:, :, None] * keys_unit.astype(jnp.float32)).astype(jnp.bfloat16)
        weighted = lax.optimization_barrier(weighted)
        key_gram = jnp.einsum('thi,thj->hij', weighted.astype(jnp.float32), keys_unit.astype(jnp.float32), precision=lax.Precision.HIGHEST)
        written = jnp.einsum('thi,thj->hij', weighted.astype(jnp.float32), values_b.astype(jnp.float32), precision=lax.Precision.HIGHEST)
        return (queries, key_gram, written)
    queries, key_gram, written = lax.map(per_frame, video_latents)
    transition, source = jax.vmap(advance, in_axes=(0, 0, 0, None))(key_gram, written, decay_rate, step_size)

    def chain_step(carried, frame_pair):
        carried = jnp.einsum('hij,hjk->hik', frame_pair[0], carried, precision=lax.Precision.HIGHEST) + frame_pair[1]
        return (carried, carried)
    initial = jnp.zeros((HEADS, DK, DK), jnp.float32)
    final_state, carried = lax.scan(chain_step, initial, (transition, source))
    head_gain = output_gain.reshape(HEADS, DK)

    def per_output(frame_pair):
        carried_b = lax.optimization_barrier(frame_pair[1].astype(jnp.bfloat16))
        readout = jnp.einsum('thi,hij->thj', frame_pair[0].astype(jnp.float32), carried_b.astype(jnp.float32), precision=lax.Precision.HIGHEST)
        scaled = readout * lax.rsqrt(lax.optimization_barrier(jnp.mean(readout * readout, axis=-1, keepdims=True)) + epsilon) * head_gain
        return scaled.astype(jnp.bfloat16).reshape(ROWS, COLS, model_width)
    return lax.map(per_output, (queries, carried))
```

```python
import functools

import jax
import jax.numpy as jnp
from jax import lax
from jax.experimental import pallas as pl
from jax.experimental.pallas import tpu as pltpu
from jax.sharding import PartitionSpec as P

MESH = pl.DeviceIdType.MESH
EPS = 1e-06
F32 = jnp.float32
BF16 = jnp.bfloat16
NX, NZ, NY = 4, 8, 8
TOKENS = 64 * 16 * 160
DK = 128
VM = pl.BlockSpec(memory_space=pltpu.VMEM)
SM = pl.BlockSpec(memory_space=pltpu.SMEM)
ANY = pl.BlockSpec(memory_space=pl.ANY)


def place():
    t, h = lax.axis_index("tm"), lax.axis_index("height")
    return lax.rem(t, NX), lax.div(h, 2), lax.div(t, NX), lax.rem(h, 2)


def dev(x, y, z, c):
    return (z * NX + x, y * 2 + c)


def up(i, d, n):
    return lax.rem(i + d, n)


def down(i, d, n):
    return lax.rem(i + n - d, n)


def rcopy(src, dst, ssem, rsem, to):
    return pltpu.make_async_remote_copy(
        src_ref=src, dst_ref=dst, send_sem=ssem, recv_sem=rsem, device_id=to, device_id_type=MESH
    )


def signal(barrier, to):
    pl.semaphore_signal(barrier, inc=1, device_id=to, device_id_type=MESH)


def mix_kernel(
    x_ref, w_ref, bw_ref, ck_ref, q_ref, g_ref,
    xe, wg, proj, kv, wt, beta, qbuf, part, got,
    s_halo, r_halo, s_ax, r_ax, s_az, r_az, s_bz, r_bz, s_bx, r_bx, s_g, r_g, s_q, r_q, l_q,
):
    x, y, z, c = place()
    xe[:, 1 + c] = x_ref[...]
    for s in range(4):
        for g in range(3):
            col = pl.multiple_of(g * 1024 + c * 512 + s * 128, 128)
            wg[s, z, x, :, g * 128 : (g + 1) * 128] = w_ref[:, pl.ds(col, 128)]

    barrier = pltpu.get_barrier_semaphore()
    signal(barrier, dev(x, y, up(z, 1, NZ), c))
    signal(barrier, dev(x, y, down(z, 1, NZ), c))
    for d in range(1, NX):
        signal(barrier, dev(up(x, d, NX), y, z, c))
    for d in range(1, NY):
        signal(barrier, dev(x, up(y, d, NY), z, c))
    signal(barrier, dev(x, up(y, 1, NY), z, 1 - c))
    signal(barrier, dev(x, down(y, 1, NY), z, 1 - c))
    signal(barrier, dev(x, y, z, 1 - c))
    pl.semaphore_wait(barrier, 15)

    ax = []
    for d in range(1, NX):
        own = wg.at[pl.ds(0, 2), z, x]
        ax.append(rcopy(own, own, s_ax.at[d - 1], r_ax.at[d - 1], dev(up(x, d, NX), y, z, c)))
        ax[-1].start()

    def ax_wait():
        for d in range(1, NX):
            src = wg.at[pl.ds(0, 2), z, down(x, d, NX)]
            rcopy(src, src, s_ax.at[d - 1], r_ax.at[d - 1], dev(x, y, z, 1 - c)).wait_recv()
        for cp in ax:
            cp.wait_send()

    zs = (dev(x, y, up(z, 1, NZ), c), dev(x, y, down(z, 1, NZ), c))

    def zblock(view, dr, k):
        zz = down(z, k, NZ) if dr == 0 else up(z, k, NZ)
        return view(zz, dr if k == 4 else None)

    def zring_send(view, ssem, rsem, k):
        for dr in range(2):
            zz = down(z, k - 1, NZ) if dr == 0 else up(z, k - 1, NZ)
            ref = view(zz, dr if k == 4 else None)
            rcopy(ref, ref, ssem.at[dr, k - 1], rsem.at[dr, k - 1], zs[dr]).start()

    def zring_recv(view, ssem, rsem, k):
        for dr in range(2):
            ref = zblock(view, dr, k)
            rcopy(ref, ref, ssem.at[dr, k - 1], rsem.at[dr, k - 1], zs[dr]).wait_recv()

    def zring_done(view, ssem, rsem):
        for k in range(1, 5):
            for dr in range(2):
                ref = zblock(view, dr, k)
                rcopy(ref, ref, ssem.at[dr, k - 1], rsem.at[dr, k - 1], zs[dr]).wait_send()

    def view_b(zz, half):
        if half is None:
            return wg.at[pl.ds(2, 2), zz, x]
        return wg.at[pl.ds(2 + half, 1), zz, x]

    def view_a(a):
        def view(zz, half):
            if half is None:
                return wg.at[a, zz]
            return wg.at[a, zz, pl.ds(2 * half, 2)]

        return view

    va = [view_a(0), view_a(1)]
    xs = (dev(up(x, 1, NX), y, z, c), dev(down(x, 1, NX), y, z, c))

    def bx_block(b, dr, k):
        xx = down(x, k, NX) if dr == 0 else up(x, k, NX)
        if k == 2:
            return wg.at[b, pl.ds(4 * dr, 4), xx]
        return wg.at[b, :, xx]

    def bx_send(i, k):
        for dr in range(2):
            xx = x if k == 1 else (down(x, 1, NX) if dr == 0 else up(x, 1, NX))
            ref = wg.at[2 + i, :, xx] if k == 1 else wg.at[2 + i, pl.ds(4 * dr, 4), xx]
            rcopy(ref, ref, s_bx.at[i, dr, k - 1], r_bx.at[i, dr, k - 1], xs[dr]).start()

    def bx_recv(i, k):
        for dr in range(2):
            ref = bx_block(2 + i, dr, k)
            rcopy(ref, ref, s_bx.at[i, dr, k - 1], r_bx.at[i, dr, k - 1], xs[dr]).wait_recv()

    def bx_done(i):
        for k in (1, 2):
            for dr in range(2):
                ref = bx_block(2 + i, dr, k)
                rcopy(ref, ref, s_bx.at[i, dr, k - 1], r_bx.at[i, dr, k - 1], xs[dr]).wait_send()

    zring_send(view_b, s_bz, r_bz, 1)

    mine = xe.at[:, 1 + c]
    theirs = xe.at[:, 2 - c]
    rcopy(mine, mine, s_halo.at[0], r_halo.at[0], dev(x, y, z, 1 - c)).start()
    for e in range(2):

        @pl.when((c == 1) & (y < NY - 1))
        def _():
            rcopy(mine, xe.at[:, 0], s_halo.at[1 + e], r_halo.at[1], dev(x, up(y, 1, NY), z, e)).start()

        @pl.when((c == 0) & (y > 0))
        def _():
            rcopy(mine, xe.at[:, 3], s_halo.at[1 + e], r_halo.at[2], dev(x, down(y, 1, NY), z, e)).start()

    @pl.when(y == 0)
    def _():
        xe[:, 0] = jnp.zeros((2, 160, 1024), BF16)

    @pl.when(y == NY - 1)
    def _():
        xe[:, 3] = jnp.zeros((2, 160, 1024), BF16)

    ax_wait()
    zring_send(va[0], s_az.at[0], r_az.at[0], 1)
    for k in (1, 2, 3):
        zring_recv(view_b, s_bz, r_bz, k)
        zring_send(view_b, s_bz, r_bz, k + 1)
        zring_recv(va[0], s_az.at[0], r_az.at[0], k)
        zring_send(va[0], s_az.at[0], r_az.at[0], k + 1)
    zring_recv(view_b, s_bz, r_bz, 4)
    bx_send(0, 1)
    zring_send(va[1], s_az.at[1], r_az.at[1], 1)

    rcopy(theirs, theirs, s_halo.at[0], r_halo.at[0], dev(x, y, z, 1 - c)).wait_recv()

    @pl.when(y > 0)
    def _():
        rcopy(mine, xe.at[:, 0], s_halo.at[1], r_halo.at[1], dev(x, y, z, 1 - c)).wait_recv()

    @pl.when(y < NY - 1)
    def _():
        rcopy(mine, xe.at[:, 3], s_halo.at[1], r_halo.at[2], dev(x, y, z, 1 - c)).wait_recv()

    for f in range(2):
        logits = jnp.dot(xe[f, 1:3].reshape(320, 1024), bw_ref[...], preferred_element_type=F32)
        gates = jax.nn.sigmoid(logits)
        gates = jnp.where(c == 0, gates[:, 0:4], gates[:, 4:8])
        for s in range(4):
            beta[f, s] = jnp.broadcast_to(gates[:, s : s + 1], (320, 128))

    def step(i, carry):
        pair, f = lax.div(i, 2), lax.rem(i, 2)
        slot = lax.rem(pair, 2) * 2 + lax.div(pair, 2)

        @pl.when(i == 0)
        def _():
            zring_recv(va[0], s_az.at[0], r_az.at[0], 4)

        @pl.when(i == 1)
        def _():
            bx_recv(0, 1)
            bx_send(0, 2)
            bx_send(1, 1)
            zring_recv(va[1], s_az.at[1], r_az.at[1], 1)
            zring_send(va[1], s_az.at[1], r_az.at[1], 2)

        @pl.when(i == 2)
        def _():
            bx_recv(0, 2)
            zring_recv(va[1], s_az.at[1], r_az.at[1], 2)
            zring_send(va[1], s_az.at[1], r_az.at[1], 3)

        @pl.when(i == 3)
        def _():
            bx_recv(1, 1)
            bx_send(1, 2)
            zring_recv(va[1], s_az.at[1], r_az.at[1], 3)
            zring_send(va[1], s_az.at[1], r_az.at[1], 4)

        @pl.when(i == 4)
        def _():
            zring_recv(va[1], s_az.at[1], r_az.at[1], 4)

        @pl.when(i == 6)
        def _():
            bx_recv(1, 2)

        proj[...] = (
            jnp.dot(
                xe[f].reshape(640, 1024), wg[slot].reshape(1024, 384), preferred_element_type=F32
            )
            .astype(BF16)
            .reshape(4, 160, 384)
        )
        ids = lax.broadcasted_iota(jnp.int32, (160, 128), 0)
        for g in range(3):
            col = pl.multiple_of(g * 1024 + (4 * c + slot) * 128, 128)
            taps = [[ck_ref[a, pl.ds(b, 1), pl.ds(col, 128)] for b in range(3)] for a in range(3)]
            for o in range(2):
                rows = [proj[o + a, :, g * 128 : (g + 1) * 128].astype(F32) for a in range(3)]
                sums = [sum(rows[a] * taps[a][b] for a in range(3)) for b in range(3)]
                total = (
                    jnp.where(ids > 0, pltpu.roll(sums[0], 1, 0), 0.0)
                    + sums[1]
                    + jnp.where(ids < 159, pltpu.roll(sums[2], 159, 0), 0.0)
                )
                s = total * jax.nn.sigmoid(total)
                if g < 2:
                    s = s * lax.rsqrt(jnp.sum(s * s, axis=-1, keepdims=True) + EPS)
                s = s.astype(BF16)
                if g == 0:
                    qbuf[slot, o, f] = s
                else:
                    kv[o * 160 : (o + 1) * 160, (g - 1) * 128 : g * 128] = s
                if g == 1:
                    wt[o * 160 : (o + 1) * 160, :] = (
                        beta[f, slot, o * 160 : (o + 1) * 160, :] * s.astype(F32)
                    ).astype(BF16)
        unit = 2 * slot + f
        part[unit] = lax.dot_general(
            wt[...], kv[...], (((0,), (0,)), ((), ())), preferred_element_type=F32
        ).astype(BF16)

        @pl.when(unit != y)
        def _():
            rcopy(part.at[unit], got.at[y], s_g.at[unit], r_g.at[y], dev(x, unit, z, c)).start()

        @pl.when(f == 1)
        def _():
            rcopy(
                qbuf.at[slot, 1 - c], q_ref.at[4 * c + slot], s_q.at[slot], r_q.at[slot], dev(x, y, z, 1 - c)
            ).start()
            pltpu.make_async_copy(qbuf.at[slot, c], q_ref.at[4 * c + slot], l_q.at[slot]).start()

        return carry

    lax.fori_loop(0, 8, step, 0)

    total = part[y].astype(F32)
    for d in range(1, NY):
        yy = up(y, d, NY)
        rcopy(got.at[yy], got.at[yy], s_g.at[0], r_g.at[yy], dev(x, y, z, 1 - c)).wait_recv()
        total = total + got[yy].astype(F32)
    g_ref[...] = total

    for s in range(4):
        dst = q_ref.at[4 * (1 - c) + s]
        cp = rcopy(qbuf.at[s, 1 - c], dst, s_q.at[s], r_q.at[s], dev(x, y, z, 1 - c))
        cp.wait_recv()
        cp.wait_send()
        pltpu.make_async_copy(qbuf.at[s, c], q_ref.at[4 * c + s], l_q.at[s]).wait()
    for u in range(8):

        @pl.when(u != y)
        def _():
            rcopy(part.at[u], got.at[y], s_g.at[u], r_g.at[y], dev(x, y, z, 1 - c)).wait_send()

    zring_done(view_b, s_bz, r_bz)
    for a in range(2):
        zring_done(va[a], s_az.at[a], r_az.at[a])
        bx_done(a)
    rcopy(mine, mine, s_halo.at[0], r_halo.at[0], dev(x, y, z, 1 - c)).wait_send()
    for e in range(2):

        @pl.when(((c == 1) & (y < NY - 1)) | ((c == 0) & (y > 0)))
        def _():
            rcopy(mine, mine, s_halo.at[1 + e], r_halo.at[1], dev(x, y, z, 1 - c)).wait_send()


def mix(latents, weight, beta_weight, conv_kernel):
    sem = pltpu.SemaphoreType.DMA
    return pl.pallas_call(
        mix_kernel,
        out_shape=(
            jax.ShapeDtypeStruct((8, 2, 160, 128), BF16),
            jax.ShapeDtypeStruct((128, 256), F32),
        ),
        in_specs=[VM] * 4,
        out_specs=(ANY, VM),
        scratch_shapes=[
            pltpu.VMEM((2, 4, 160, 1024), BF16),
            pltpu.VMEM((4, NZ, NX, 32, 384), BF16),
            pltpu.VMEM((4, 160, 384), BF16),
            pltpu.VMEM((320, 256), BF16),
            pltpu.VMEM((320, 128), BF16),
            pltpu.VMEM((2, 4, 320, 128), F32),
            pltpu.VMEM((4, 2, 2, 160, 128), BF16),
            pltpu.VMEM((8, 128, 256), BF16),
            pltpu.VMEM((8, 128, 256), BF16),
            sem((3,)), sem((3,)),
            sem((3,)), sem((3,)),
            sem((2, 2, 4)), sem((2, 2, 4)),
            sem((2, 4)), sem((2, 4)),
            sem((2, 2, 2)), sem((2, 2, 2)),
            sem((8,)), sem((8,)),
            sem((4,)), sem((4,)), sem((4,)),
        ],
        compiler_params=pltpu.CompilerParams(
            collective_id=0, has_side_effects=True, vmem_limit_bytes=40 * 2**20
        ),
        name="mix",
    )(latents, weight, beta_weight, conv_kernel)


def exact(a, b):
    return jnp.dot(a, b, preferred_element_type=F32, precision=lax.Precision.HIGHEST)


def inverse(system):
    ident = (
        lax.broadcasted_iota(jnp.int32, (DK, DK), 0) == lax.broadcasted_iota(jnp.int32, (DK, DK), 1)
    ).astype(F32)
    power = ident - 0.4 * system
    total = ident + power
    for _ in range(4):
        power = exact(power, power)
        total = total + exact(total, power)
    return 0.4 * total


def chain_kernel(
    g_ref, rate_ref, decay_ref, st_ref,
    own, fin, px, zmap, zin, ein, cb, st,
    s_f, r_f, s_x, r_x, s_z, r_z, s_e, r_e, s_st, r_st, s_sib, r_sib, l_st,
):
    x, y, z, c = place()
    f, head = lax.rem(y, 2), 4 * c + lax.div(y, 2)
    barrier = pltpu.get_barrier_semaphore()
    for d in range(1, NX):
        signal(barrier, dev(up(x, d, NX), y, z, c))
    for d in range(1, NY):
        signal(barrier, dev(x, up(y, d, NY), z, c))
    for d in range(1, NZ):
        signal(barrier, dev(x, y, up(z, d, NZ), c))
    signal(barrier, dev(x, y, z, 1 - c))

    step_size = rate_ref[head] * (DK / TOKENS)
    retain = jnp.exp(-jnp.full((DK, DK), decay_ref[f, head], F32))
    gram, written = g_ref[:, :DK], g_ref[:, DK:]
    diagonal = lax.broadcasted_iota(jnp.int32, (DK, DK), 0) == lax.broadcasted_iota(
        jnp.int32, (DK, DK), 1
    )
    system = jnp.where(diagonal, 1.0, 0.0) + (0.5 * step_size) * (gram + gram.T)
    solved = inverse(system)
    transition = retain * solved
    source = retain * exact(solved, step_size * written)
    own[:, :DK] = transition.astype(BF16)
    own[:, DK:] = source.astype(BF16)

    def compose(latter, earlier):
        both = jnp.dot(latter[:, :DK], earlier, preferred_element_type=F32)
        return jnp.concatenate([both[:, :DK], both[:, DK:] + latter[:, DK:].astype(F32)], axis=1).astype(BF16)

    pl.semaphore_wait(barrier, 18)

    pair = rcopy(own, fin, s_f, r_f, dev(x, y + 1 - 2 * f, z, c))
    pair.start()
    pair.wait_recv()
    mine, other = own[...], fin[...]
    both = compose(jnp.where(f == 0, other, mine), jnp.where(f == 0, mine, other))
    px[x] = both
    for d in range(1, NX):
        rcopy(px.at[x], px.at[x], s_x.at[d - 1], r_x.at[d - 1], dev(up(x, d, NX), y, z, c)).start()
    for d in range(1, NX):
        src = px.at[down(x, d, NX)]
        rcopy(src, src, s_x.at[d - 1], r_x.at[d - 1], dev(x, y, z, 1 - c)).wait_recv()
    first = compose(px[1], px[0])
    zmap[0] = compose(compose(px[3], px[2]), first)
    odd, late, last = lax.rem(z, 2) == 1, lax.rem(z, 4) >= 2, z >= 4

    @pl.when(jnp.logical_not(odd))
    def _():
        rcopy(zmap.at[0], zin.at[0], s_z.at[0], r_z.at[0], dev(x, y, z + 1, c)).start()

    third = compose(px[2], first)
    current = jnp.where(f == 0, mine, both)
    before = jnp.where(x == 1, px[0], jnp.where(x == 2, first, third))
    before = compose(current, before)
    own_map = jnp.where(x == 0, current, before)

    fin2 = zmap.at[2]
    fin2[...] = own_map

    @pl.when(odd)
    def _():
        rcopy(zmap.at[0], zin.at[0], s_z.at[0], r_z.at[0], dev(x, y, z, 1 - c)).wait_recv()
        zmap[1] = compose(zmap[0], zin[0])

    @pl.when(jnp.logical_not(odd))
    def _():
        zmap[1] = zmap[0]

    sends2 = lax.rem(z, 4) == 1
    for e in range(2):

        @pl.when(sends2)
        def _():
            rcopy(zmap.at[1], zin.at[1], s_z.at[1 + e], r_z.at[1], dev(x, y, z + 1 + e, c)).start()

    @pl.when(odd)
    def _():
        fin2[...] = compose(fin2[...], zin[0])

    @pl.when(late)
    def _():
        rcopy(zmap.at[1], zin.at[1], s_z.at[1], r_z.at[1], dev(x, y, z, 1 - c)).wait_recv()

    @pl.when(z == 3)
    def _():
        ein[0] = compose(zmap[1], zin[1])[:, DK:]
        for e in range(4):
            rcopy(ein.at[0], ein.at[1], s_e.at[e], r_e, dev(x, y, 4 + e, c)).start()

    @pl.when(late)
    def _():
        fin2[...] = compose(fin2[...], zin[1])

    @pl.when(last)
    def _():
        rcopy(ein.at[0], ein.at[1], s_e.at[0], r_e, dev(x, y, z, 1 - c)).wait_recv()
        m = fin2[...]
        cb[...] = (
            jnp.dot(m[:, :DK], ein[1], preferred_element_type=F32) + m[:, DK:].astype(F32)
        ).astype(BF16)

    @pl.when(jnp.logical_not(last))
    def _():
        cb[...] = fin2[:, DK:]

    st[c, y] = cb[...]
    rcopy(st.at[c, y], st.at[c, y], s_sib.at[y], r_sib.at[y], dev(x, y, z, 1 - c)).start()
    for d in range(1, NY):
        rcopy(cb, st.at[c, y], s_st.at[d - 1], r_st.at[d - 1], dev(x, up(y, d, NY), z, c)).start()
    for d in (1, 7, 2, 6, 3, 5, 4):
        yy = down(y, d, NY)
        rcopy(cb, st.at[c, yy], s_st.at[d - 1], r_st.at[d - 1], dev(x, y, z, 1 - c)).wait_recv()
        rcopy(st.at[c, yy], st.at[c, yy], s_sib.at[yy], r_sib.at[yy], dev(x, y, z, 1 - c)).start()
    mine_out = pltpu.make_async_copy(st.at[c], st_ref.at[c], l_st.at[0])
    mine_out.start()
    for k in range(NY):
        rcopy(st.at[1 - c, k], st.at[1 - c, k], s_sib.at[k], r_sib.at[k], dev(x, y, z, 1 - c)).wait_recv()
    other_out = pltpu.make_async_copy(st.at[1 - c], st_ref.at[1 - c], l_st.at[1])
    other_out.start()

    pair.wait_send()
    for d in range(1, NX):
        rcopy(px.at[x], px.at[x], s_x.at[d - 1], r_x.at[d - 1], dev(x, y, z, 1 - c)).wait_send()

    @pl.when(jnp.logical_not(odd))
    def _():
        rcopy(zmap.at[0], zin.at[0], s_z.at[0], r_z.at[0], dev(x, y, z, 1 - c)).wait_send()

    for e in range(2):

        @pl.when(sends2)
        def _():
            rcopy(zmap.at[1], zin.at[1], s_z.at[1 + e], r_z.at[1], dev(x, y, z, 1 - c)).wait_send()

    @pl.when(z == 3)
    def _():
        for e in range(4):
            rcopy(ein.at[0], ein.at[1], s_e.at[e], r_e, dev(x, y, z, 1 - c)).wait_send()

    for d in range(1, NY):
        rcopy(cb, st.at[c, y], s_st.at[d - 1], r_st.at[d - 1], dev(x, y, z, 1 - c)).wait_send()
    for k in range(NY):
        rcopy(st.at[c, k], st.at[c, k], s_sib.at[k], r_sib.at[k], dev(x, y, z, 1 - c)).wait_send()
    mine_out.wait()
    other_out.wait()


def chain(gram, step_rate, decay_rate):
    sem = pltpu.SemaphoreType.DMA
    return pl.pallas_call(
        chain_kernel,
        out_shape=jax.ShapeDtypeStruct((2, NY, DK, DK), BF16),
        in_specs=[VM, SM, SM],
        out_specs=ANY,
        scratch_shapes=[
            pltpu.VMEM((DK, 2 * DK), BF16),
            pltpu.VMEM((DK, 2 * DK), BF16),
            pltpu.VMEM((NX, DK, 2 * DK), BF16),
            pltpu.VMEM((3, DK, 2 * DK), BF16),
            pltpu.VMEM((2, DK, 2 * DK), BF16),
            pltpu.VMEM((2, DK, DK), BF16),
            pltpu.VMEM((DK, DK), BF16),
            pltpu.VMEM((2, NY, DK, DK), BF16),
            sem(()), sem(()),
            sem((3,)), sem((3,)),
            sem((3,)), sem((2,)),
            sem((4,)), sem(()),
            sem((7,)), sem((7,)),
            sem((8,)), sem((8,)),
            sem((2,)),
        ],
        compiler_params=pltpu.CompilerParams(
            collective_id=1, has_side_effects=True, vmem_limit_bytes=32 * 2**20
        ),
        name="chain",
    )(gram, step_rate, decay_rate)


def read_kernel(q_ref, st_ref, gain_ref, o_ref):
    for f in range(2):
        for head in range(8):
            state = st_ref[head // 4, 2 * (head % 4) + f]
            r = jnp.dot(q_ref[head, f], state, preferred_element_type=F32)
            r = r * lax.rsqrt(jnp.mean(r * r, axis=-1, keepdims=True) + EPS)
            r = r * gain_ref[:, head * DK : (head + 1) * DK]
            o_ref[f, 0, :, head * DK : (head + 1) * DK] = r.astype(BF16)


def read(queries, states, gain):
    return pl.pallas_call(
        read_kernel,
        out_shape=jax.ShapeDtypeStruct((2, 1, 160, 1024), BF16),
        in_specs=[VM] * 3,
        out_specs=VM,
        compiler_params=pltpu.CompilerParams(vmem_limit_bytes=32 * 2**20),
        name="read",
    )(queries, states, gain)


def body(video_latents, qkv_weight, beta_weight, conv_kernel, decay_rate, step_rate, output_gain):
    queries, gram = mix(video_latents.reshape(2, 160, 1024), qkv_weight, beta_weight, conv_kernel)
    states = chain(gram, step_rate, decay_rate)
    return read(queries, states, output_gain.reshape(1, 1024))


def solution(mesh):
    placed = (P("tm", "height", None, None), P("tm", None), P(), P(), P("tm", None), P(), P())
    return jax.shard_map(
        body, mesh=mesh, in_specs=placed, out_specs=P("tm", "height", None, None), check_vma=False
    )
```

```python
import functools

import jax
import jax.numpy as jnp
from jax import lax
from jax.experimental import pallas as pl
from jax.experimental.pallas import tpu as pltpu
from jax.sharding import PartitionSpec as P

MESH = pl.DeviceIdType.MESH
EPS = 1e-06
F32 = jnp.float32
BF16 = jnp.bfloat16
NX, NZ, NY = 4, 8, 8
TOKENS = 64 * 16 * 160
DK = 128
VM = pl.BlockSpec(memory_space=pltpu.VMEM)
SM = pl.BlockSpec(memory_space=pltpu.SMEM)
ANY = pl.BlockSpec(memory_space=pl.ANY)


def place():
    t, h = lax.axis_index("tm"), lax.axis_index("height")
    return lax.rem(t, NX), lax.div(h, 2), lax.div(t, NX), lax.rem(h, 2)


def dev(x, y, z, c):
    return (z * NX + x, y * 2 + c)


def up(i, d, n):
    return lax.rem(i + d, n)


def down(i, d, n):
    return lax.rem(i + n - d, n)


def rcopy(src, dst, ssem, rsem, to):
    return pltpu.make_async_remote_copy(
        src_ref=src, dst_ref=dst, send_sem=ssem, recv_sem=rsem, device_id=to, device_id_type=MESH
    )


def signal(barrier, to):
    pl.semaphore_signal(barrier, inc=1, device_id=to, device_id_type=MESH)


def exact(a, b):
    return jnp.dot(a, b, preferred_element_type=F32, precision=lax.Precision.HIGHEST)


def inverse(system):
    ident = (
        lax.broadcasted_iota(jnp.int32, (DK, DK), 0) == lax.broadcasted_iota(jnp.int32, (DK, DK), 1)
    ).astype(F32)
    power = ident - 0.4 * system
    total = ident + power
    for _ in range(4):
        power = exact(power, power)
        total = total + exact(total, power)
    return 0.4 * total


def mix_kernel(
    x_ref, w_ref, bw_ref, ck_hbm, rate_ref, decay_ref, q_ref, st_ref,
    xe, wg, ck_ref, proj, kv, wt, beta, qbuf, part, got, own, fin, px, zin, state, cb, st,
    s_row, r_row, s_fwd, r_fwd, s_ax, r_ax, s_az, r_az, s_bz, r_bz, s_bx, r_bx, s_g, r_g, s_q, r_q, l_q, l_in,
    s_f, r_f, s_x, r_x, s_z, r_z, s_zs, r_zs, s_st, r_st, s_sib, r_sib, l_st,
):
    x, y, z, c = place()
    par, half_y = lax.rem(y, 2), lax.div(y, 2)
    sibling = dev(x, y, z, 1 - c)
    ynext, yprev = up(y, 1, NY), down(y, 1, NY)

    loads = [pltpu.make_async_copy(x_ref.at[f], xe.at[f, 2 + c], l_in.at[f]) for f in range(2)]
    for s in range(2):
        for g in range(3):
            col = pl.multiple_of(g * 1024 + (4 * par + 2 * c + s) * 128, 128)
            loads.append(
                pltpu.make_async_copy(
                    w_ref.at[:, pl.ds(col, 128)], wg.at[s, z, x, :, pl.ds(g * 128, 128)], l_in.at[2 + 3 * s + g]
                )
            )
    taps_in = pltpu.make_async_copy(ck_hbm, ck_ref, l_in.at[8])
    for cp in loads:
        cp.start()
    taps_in.start()

    barrier = pltpu.get_barrier_semaphore()
    for d in range(1, NZ):
        signal(barrier, dev(x, y, up(z, d, NZ), c))
    for d in range(1, NX):
        signal(barrier, dev(up(x, d, NX), y, z, c))
    for d in range(1, NY):
        for e in range(2):
            signal(barrier, dev(x, up(y, d, NY), z, e))
    signal(barrier, sibling)
    for cp in loads:
        cp.wait()
    pl.semaphore_wait(barrier, 25)

    zs = (dev(x, y, up(z, 1, NZ), c), dev(x, y, down(z, 1, NZ), c))

    def zsrc(dr, k):
        return down(z, k, NZ) if dr == 0 else up(z, k, NZ)

    def b_view(zz, k, dr):
        return wg.at[1, zz, x, pl.ds(16 * dr, 16)] if k == 4 else wg.at[1, zz, x]

    def b_copy(dr, k, sending):
        ref = b_view(zsrc(dr, k - 1 if sending else k), k, dr)
        return rcopy(ref, ref, s_bz.at[dr, k - 1], r_bz.at[dr, k - 1], zs[dr])

    def a_copy(dr, hf, k, sending):
        ref = wg.at[0, zsrc(dr, k - 1 if sending else k), pl.ds(2 * hf, 2)]
        return rcopy(ref, ref, s_az.at[dr, hf, k - 1], r_az.at[dr, hf, k - 1], zs[dr])

    def ax_copy(d, xx):
        ref = wg.at[0, z, xx]
        return rcopy(ref, ref, s_ax.at[d - 1], r_ax.at[d - 1], dev(up(x, d, NX), y, z, c))

    def bx_copy(d, zz, xx):
        ref = wg.at[1, zz, xx]
        return rcopy(ref, ref, s_bx.at[d - 1, zz], r_bx.at[d - 1, zz], dev(up(x, d, NX), y, z, c))

    def bx_start(zz):
        for d in (2, 1, 3):
            bx_copy(d, zz, x).start()

    for dr in range(2):
        b_copy(dr, 1, True).start()
    for d in (2, 1, 3):
        ax_copy(d, x).start()

    def row_copy(f, dr):
        to = dev(x, ynext, z, c) if dr == 0 else dev(x, yprev, z, c)
        return rcopy(xe.at[f, 2 + c], xe.at[f, 4 * dr + c], s_row.at[f, dr], r_row.at[f, dr], to)

    def fwd_copy(f, k, sending):
        core = c if sending else 1 - c
        ref = xe.at[f, 2 * k + core]
        return rcopy(ref, ref, s_fwd.at[f, k], r_fwd.at[f, k], sibling)

    for f in range(2):
        for dr in range(2):
            row_copy(f, dr).start()
    for f in range(2):
        fwd_copy(f, 1, True).start()
    bx_start(z)

    def rows_forward(f):
        for dr in range(2):
            row_copy(f, dr).wait_recv()
            fwd_copy(f, 2 * dr, True).start()

    def rows_wait(f):
        for k in range(3):
            fwd_copy(f, k, False).wait_recv()

    for d in range(1, NX):
        ax_copy(d, down(x, d, NX)).wait_recv()
    for hf in range(2):
        for dr in range(2):
            a_copy(dr, hf, 1, True).start()

    def hop(k):
        for dr in range(2):
            b_copy(dr, k, False).wait_recv()
            b_copy(dr, k + 1, True).start()
        for dr in range(2):
            bx_start(zsrc(dr, k))
        for hf in range(2):
            for dr in range(2):
                a_copy(dr, hf, k, False).wait_recv()
                if k < 3 or hf == dr:
                    a_copy(dr, hf, k + 1, True).start()

    hop(1)
    hop(2)
    rows_forward(0)
    hop(3)
    for dr in range(2):
        b_copy(dr, 4, False).wait_recv()
    bx_start(zsrc(0, 4))

    taps_in.wait()

    def gates_of(f):
        logits = lax.dot_general(
            xe[f, 1:5].reshape(640, 1024), bw_ref[...], (((1,), (1,)), ((), ())), preferred_element_type=F32
        )
        gates = jax.nn.sigmoid(logits)
        lanes = lax.broadcasted_iota(jnp.int32, (640, 8), 1)
        for s in range(2):
            picked = jnp.where(lanes == 4 * par + 2 * c + s, gates, 0.0)
            beta[f, s] = jnp.broadcast_to(jnp.sum(picked, axis=1, keepdims=True), (640, 128))

    rows_wait(0)
    gates_of(0)
    for d in range(1, NX):
        for k in range(NZ):
            bx_copy(d, k, down(x, d, NX)).wait_recv()

    low = jnp.where(y == 0, 0.0, 1.0).astype(F32)
    high = jnp.where(y == NY - 1, 0.0, 1.0).astype(F32)

    def unit_owner(slot, f):
        j = 2 * c + slot
        return 2 * j + par, f

    def step(i, carry):
        f, slot = lax.div(i, 2), 1 - lax.rem(i, 2)

        @pl.when(i == 1)
        def _():
            for dr in range(2):
                a_copy(dr, dr, 4, False).wait_recv()
            rows_forward(1)

        @pl.when(i == 2)
        def _():
            rows_wait(1)
            gates_of(1)

        proj[...] = (
            jnp.dot(
                xe[f].reshape(960, 1024), wg[slot].reshape(1024, 384), preferred_element_type=F32
            )
            .astype(BF16)
            .reshape(6, 160, 384)
        )
        ids = lax.broadcasted_iota(jnp.int32, (160, 128), 0)
        for g in range(3):
            col = pl.multiple_of(g * 1024 + (4 * par + 2 * c + slot) * 128, 128)
            taps = [[ck_ref[a, pl.ds(b, 1), pl.ds(col, 128)] for b in range(3)] for a in range(3)]
            for o in range(4):
                scale = {(0, 2): low, (1, 0): low, (2, 2): high, (3, 0): high}
                rows = [proj[o + a, :, g * 128 : (g + 1) * 128].astype(F32) for a in range(3)]
                sums = [
                    sum(
                        rows[a] * (taps[a][b] * scale[(o, a)] if (o, a) in scale else taps[a][b])
                        for a in range(3)
                    )
                    for b in range(3)
                ]
                total = (
                    jnp.where(ids > 0, pltpu.roll(sums[0], 1, 0), 0.0)
                    + sums[1]
                    + jnp.where(ids < 159, pltpu.roll(sums[2], 159, 0), 0.0)
                )
                s = total * jax.nn.sigmoid(total)
                if g < 2:
                    s = s * lax.rsqrt(jnp.sum(s * s, axis=-1, keepdims=True) + EPS)
                s = s.astype(BF16)
                if g == 0:
                    qbuf[slot, o, f] = s
                else:
                    kv[o * 160 : (o + 1) * 160, (g - 1) * 128 : g * 128] = s
                if g == 1:
                    wt[o * 160 : (o + 1) * 160, :] = (
                        beta[f, slot, o * 160 : (o + 1) * 160, :] * s.astype(F32)
                    ).astype(BF16)
        unit = lax.dot_general(
            wt[...], kv[...], (((0,), (0,)), ((), ())), preferred_element_type=F32
        ).astype(BF16)
        part[slot, f] = unit
        owner, core = unit_owner(slot, f)
        here = (owner == y) & (core == c)

        @pl.when(here)
        def _():
            got[half_y] = unit

        @pl.when(jnp.logical_not(here))
        def _():
            rcopy(
                part.at[slot, f], got.at[half_y], s_g.at[slot, f], r_g.at[half_y], dev(x, owner, z, core)
            ).start()

        return carry

    lax.fori_loop(0, 4, step, 0)

    def q_out(slot, o, send):
        head = 4 * par + 2 * c + slot
        to = {0: dev(x, yprev, z, 1), 1: dev(x, y, z, 0), 2: dev(x, y, z, 1), 3: dev(x, ynext, z, 0)}[o]

        def act(cp, local):
            if send:
                cp.start()
            elif local:
                cp.wait()
            else:
                cp.wait_send()

        far = rcopy(qbuf.at[slot, o], q_ref.at[head], s_q.at[slot, o], r_q.at[head], to)
        if o in (0, 3):
            act(far, False)
            return

        @pl.when(c == o - 1)
        def _():
            act(pltpu.make_async_copy(qbuf.at[slot, o], q_ref.at[head], l_q.at[slot]), True)

        @pl.when(c != o - 1)
        def _():
            act(far, False)

    for slot in range(2):
        for o in (0, 3, 1, 2):
            q_out(slot, o, True)

    step_size = rate_ref[4 * par + half_y] * (DK / TOKENS)
    retain = jnp.exp(-jnp.full((DK, DK), decay_ref[c, 4 * par + half_y], F32))
    summed = None
    for k in range(4):
        source_is_here = (k == half_y) & (lax.div(half_y, 2) == c)

        @pl.when(jnp.logical_not(source_is_here))
        def _():
            rcopy(got.at[k], got.at[k], s_g.at[0, 0], r_g.at[k], sibling).wait_recv()

        summed = got[k].astype(F32) if summed is None else summed + got[k].astype(F32)
    gram, written = summed[:, :DK], summed[:, DK:]
    diagonal = lax.broadcasted_iota(jnp.int32, (DK, DK), 0) == lax.broadcasted_iota(
        jnp.int32, (DK, DK), 1
    )
    system = jnp.where(diagonal, 1.0, 0.0) + (0.5 * step_size) * (gram + gram.T)
    solved = inverse(system)
    own[:, :DK] = (retain * solved).astype(BF16)
    own[:, DK:] = (retain * exact(solved, step_size * written)).astype(BF16)

    def compose(latter, earlier):
        both = jnp.dot(latter[:, :DK], earlier, preferred_element_type=F32)
        return jnp.concatenate([both[:, :DK], both[:, DK:] + latter[:, DK:].astype(F32)], axis=1).astype(BF16)

    pair = rcopy(own, fin, s_f, r_f, sibling)
    pair.start()
    pair.wait_recv()
    mine, other = own[...], fin[...]
    both = compose(jnp.where(c == 0, other, mine), jnp.where(c == 0, mine, other))
    px[x] = both

    def px_copy(d, xx):
        return rcopy(px.at[xx], px.at[xx], s_x.at[d - 1], r_x.at[d - 1], dev(up(x, d, NX), y, z, c))

    for d in (2, 1, 3):
        px_copy(d, x).start()
    for d in (1, 3, 2):
        px_copy(d, down(x, d, NX)).wait_recv()
    first = compose(px[1], px[0])
    line = compose(compose(px[3], px[2]), first)
    zin[0, z] = line[:, :DK]
    zin[1, z] = line[:, DK:]

    def z_copy(e):
        return rcopy(zin.at[c, z], zin.at[c, z], s_z.at[e - 1], r_z.at[z], dev(x, y, z + e, c))

    def zs_copy(k, sending):
        core = c if sending else 1 - c
        return rcopy(zin.at[core, k], zin.at[core, k], s_zs.at[k], r_zs.at[k], sibling)

    for e in range(NZ - 1, 0, -1):

        @pl.when(z + e < NZ)
        def _():
            z_copy(e).start()

    third = compose(px[2], first)
    current = jnp.where(c == 0, mine, both)
    before = jnp.where(x == 1, px[0], jnp.where(x == 2, first, third))
    fin[...] = jnp.where(x == 0, current, compose(current, before))

    for e in range(1, NZ):

        @pl.when(z >= e)
        def _():
            k = z - e
            rcopy(zin.at[c, k], zin.at[c, k], s_z.at[0], r_z.at[k], sibling).wait_recv()
            zs_copy(k, True).start()

    for k in range(NZ - 1):

        @pl.when(k < z)
        def _():
            zs_copy(k, False).wait_recv()
            if k == 0:
                state[...] = zin[1, 0].astype(F32)
            else:
                state[...] = jnp.dot(
                    zin[0, k], state[...].astype(BF16), preferred_element_type=F32
                ) + zin[1, k].astype(F32)

    @pl.when(z == 0)
    def _():
        cb[...] = fin[:, DK:]

    @pl.when(z > 0)
    def _():
        cb[...] = (
            jnp.dot(fin[:, :DK], state[...].astype(BF16), preferred_element_type=F32)
            + fin[:, DK:].astype(F32)
        ).astype(BF16)

    def sib_copy(k, sending):
        core = c if sending else 1 - c
        return rcopy(st.at[core, k], st.at[core, k], s_sib.at[k], r_sib.at[k], sibling)

    def st_copy(d, yy):
        return rcopy(cb, st.at[c, yy], s_st.at[d - 1], r_st.at[d - 1], dev(x, up(y, d, NY), z, c))

    for d in (4, 3, 5, 2, 6, 1, 7):
        st_copy(d, y).start()
    st[c, y] = cb[...]
    sib_copy(y, True).start()
    for d in (1, 7, 2, 6, 3, 5, 4):
        yy = down(y, d, NY)
        st_copy(d, yy).wait_recv()
        sib_copy(yy, True).start()
    mine_out = pltpu.make_async_copy(st.at[c], st_ref.at[c], l_st.at[0])
    mine_out.start()
    for k in range(NY):
        sib_copy(k, False).wait_recv()
    other_out = pltpu.make_async_copy(st.at[1 - c], st_ref.at[1 - c], l_st.at[1])
    other_out.start()

    for slot in range(2):
        for o in range(4):
            q_out(slot, o, False)
        head = 4 * par + 2 * (1 - c) + slot
        rcopy(qbuf.at[slot, 0], q_ref.at[head], s_q.at[slot, 0], r_q.at[head], sibling).wait_recv()
    for k in range(4):
        head = 4 * (1 - par) + k
        rcopy(qbuf.at[0, 0], q_ref.at[head], s_q.at[0, 0], r_q.at[head], sibling).wait_recv()
    for slot in range(2):
        for f in range(2):
            owner, core = unit_owner(slot, f)

            @pl.when(jnp.logical_not((owner == y) & (core == c)))
            def _():
                rcopy(part.at[slot, f], got.at[0], s_g.at[slot, f], r_g.at[0], sibling).wait_send()

    for dr in range(2):
        for k in range(1, 5):
            b_copy(dr, k, True).wait_send()
            for hf in range(2):
                if k < 4 or hf == dr:
                    a_copy(dr, hf, k, True).wait_send()
    for d in range(1, NX):
        ax_copy(d, x).wait_send()
        px_copy(d, x).wait_send()
        for k in range(NZ):
            bx_copy(d, k, x).wait_send()
    for f in range(2):
        for dr in range(2):
            row_copy(f, dr).wait_send()
        for k in range(3):
            fwd_copy(f, k, True).wait_send()
    pair.wait_send()
    for e in range(1, NZ):

        @pl.when(z + e < NZ)
        def _():
            z_copy(e).wait_send()

    for k in range(NZ - 1):

        @pl.when(k < z)
        def _():
            zs_copy(k, True).wait_send()

    for d in range(1, NY):
        st_copy(d, y).wait_send()
    for k in range(NY):
        sib_copy(k, True).wait_send()
    mine_out.wait()
    other_out.wait()


def mix(latents, weight, beta_rows, conv_kernel, step_rate, decay_rate):
    sem = pltpu.SemaphoreType.DMA
    return pl.pallas_call(
        mix_kernel,
        out_shape=(
            jax.ShapeDtypeStruct((8, 2, 160, DK), BF16),
            jax.ShapeDtypeStruct((2, NY, DK, DK), BF16),
        ),
        in_specs=[ANY, ANY, VM, ANY, SM, SM],
        out_specs=(ANY, ANY),
        scratch_shapes=[
            pltpu.VMEM((2, 6, 160, 1024), BF16),
            pltpu.VMEM((2, NZ, NX, 32, 384), BF16),
            pltpu.VMEM((3, 3, 3072), F32),
            pltpu.VMEM((6, 160, 384), BF16),
            pltpu.VMEM((640, 256), BF16),
            pltpu.VMEM((640, DK), BF16),
            pltpu.VMEM((2, 2, 640, DK), F32),
            pltpu.VMEM((2, 4, 2, 160, DK), BF16),
            pltpu.VMEM((2, 2, DK, 2 * DK), BF16),
            pltpu.VMEM((4, DK, 2 * DK), BF16),
            pltpu.VMEM((DK, 2 * DK), BF16),
            pltpu.VMEM((DK, 2 * DK), BF16),
            pltpu.VMEM((NX, DK, 2 * DK), BF16),
            pltpu.VMEM((2, NZ, DK, DK), BF16),
            pltpu.VMEM((DK, DK), F32),
            pltpu.VMEM((DK, DK), BF16),
            pltpu.VMEM((2, NY, DK, DK), BF16),
            sem((2, 2)), sem((2, 2)), sem((2, 3)), sem((2, 3)),
            sem((3,)), sem((3,)), sem((2, 2, 4)), sem((2, 2, 4)),
            sem((2, 4)), sem((2, 4)), sem((3, 8)), sem((3, 8)),
            sem((2, 2)), sem((4,)), sem((2, 4)), sem((8,)), sem((2,)), sem((9,)),
            sem(()), sem(()), sem((3,)), sem((3,)),
            sem((7,)), sem((8,)), sem((8,)), sem((8,)),
            sem((7,)), sem((7,)), sem((8,)), sem((8,)), sem((2,)),
        ],
        compiler_params=pltpu.CompilerParams(
            collective_id=0, has_side_effects=True, vmem_limit_bytes=56 * 2**20
        ),
        name="mix",
    )(latents, weight, beta_rows, conv_kernel, step_rate, decay_rate)


def read_kernel(q_ref, st_ref, gain_ref, o_ref):
    for f in range(2):
        for head in range(8):
            state = st_ref[f, 2 * (head % 4) + head // 4]
            r = jnp.dot(q_ref[head, f], state, preferred_element_type=F32)
            r = r * lax.rsqrt(jnp.mean(r * r, axis=-1, keepdims=True) + EPS)
            r = r * gain_ref[:, head * DK : (head + 1) * DK]
            o_ref[f, 0, :, head * DK : (head + 1) * DK] = r.astype(BF16)


def read(queries, states, gain):
    return pl.pallas_call(
        read_kernel,
        out_shape=jax.ShapeDtypeStruct((2, 1, 160, 1024), BF16),
        in_specs=[VM] * 3,
        out_specs=VM,
        compiler_params=pltpu.CompilerParams(vmem_limit_bytes=32 * 2**20),
        name="read",
    )(queries, states, gain)


def body(video_latents, qkv_weight, beta_weight, conv_kernel, decay_rate, step_rate, output_gain):
    queries, states = mix(
        video_latents.reshape(2, 160, 1024), qkv_weight, beta_weight.T, conv_kernel, step_rate, decay_rate
    )
    return read(queries, states, output_gain.reshape(1, 1024))


def solution(mesh):
    placed = (P("tm", "height", None, None), P("tm", None), P(), P(), P("tm", None), P(), P())
    return jax.shard_map(
        body, mesh=mesh, in_specs=placed, out_specs=P("tm", "height", None, None), check_vma=False
    )
```

```python
import functools

import jax
import jax.numpy as jnp
from jax import lax
from jax.experimental import pallas as pl
from jax.experimental.pallas import tpu as pltpu
from jax.sharding import PartitionSpec as P

MESH = pl.DeviceIdType.MESH
EPS = 1e-06
F32 = jnp.float32
BF16 = jnp.bfloat16
NX, NZ, NY = 4, 8, 8
TOKENS = 64 * 16 * 160
DK = 128
VM = pl.BlockSpec(memory_space=pltpu.VMEM)
SM = pl.BlockSpec(memory_space=pltpu.SMEM)
ANY = pl.BlockSpec(memory_space=pl.ANY)


def place():
    t, h = lax.axis_index("tm"), lax.axis_index("height")
    return lax.rem(t, NX), lax.div(h, 2), lax.div(t, NX), lax.rem(h, 2)


def dev(x, y, z, c):
    return (z * NX + x, y * 2 + c)


def up(i, d, n):
    return lax.rem(i + d, n)


def down(i, d, n):
    return lax.rem(i + n - d, n)


def rcopy(src, dst, ssem, rsem, to):
    return pltpu.make_async_remote_copy(
        src_ref=src, dst_ref=dst, send_sem=ssem, recv_sem=rsem, device_id=to, device_id_type=MESH
    )


def signal(barrier, to):
    pl.semaphore_signal(barrier, inc=1, device_id=to, device_id_type=MESH)


def halves(a):
    high = a.astype(BF16)
    return high, (a - high.astype(F32)).astype(BF16)


def close(a, b):
    a_high, a_low = halves(a)
    b_high, b_low = halves(b)
    both = jnp.concatenate([a_high, a_low], axis=1)
    return jnp.dot(
        both, jnp.concatenate([b_high, b_high], axis=0), preferred_element_type=F32
    ) + jnp.dot(a_high, b_low, preferred_element_type=F32)


def inverse(system, ident):
    power = ident - 0.4 * system
    total = ident + power
    power = close(power, power)
    for _ in range(3):
        stacked = close(jnp.concatenate([power, total], axis=0), power)
        power, total = stacked[:DK], total + stacked[DK:]
    return 0.4 * (total + close(total, power))


def mix_kernel(
    x_ref, w_ref, bw_ref, ck_hbm, gain_ref, rate_ref, decay_ref, o_ref,
    xe, wg, ck_ref, proj, kv, wt, beta, qbuf, q_ref, part, got, own, fin, px, zin, state, cb, st,
    s_row, r_row, s_fwd, r_fwd, s_wz, r_wz, s_wx, r_wx, s_g, r_g, s_q, r_q, l_q, l_in,
    s_f, r_f, s_x, r_x, s_z, r_z, s_zs, r_zs, s_st, r_st, s_sib, r_sib,
):
    x, y, z, c = place()
    par, half_y = lax.rem(y, 2), lax.div(y, 2)
    sibling = dev(x, y, z, 1 - c)
    ynext, yprev = up(y, 1, NY), down(y, 1, NY)

    loads = [pltpu.make_async_copy(x_ref.at[f], xe.at[f, 2 + c], l_in.at[f]) for f in range(2)]
    for s in range(2):
        for g in range(3):
            col = pl.multiple_of(g * 1024 + (4 * par + 2 * c + s) * 128, 128)
            block, lane = (2, s * 128) if g == 0 else (s, (g - 1) * 128)
            loads.append(
                pltpu.make_async_copy(
                    w_ref.at[:, pl.ds(col, 128)], wg.at[block, z, x, :, pl.ds(lane, 128)], l_in.at[2 + 3 * s + g]
                )
            )
    taps_in = pltpu.make_async_copy(ck_hbm, ck_ref, l_in.at[8])
    for cp in loads:
        cp.start()
    taps_in.start()

    barrier = pltpu.get_barrier_semaphore()
    for d in range(1, NZ):
        signal(barrier, dev(x, y, up(z, d, NZ), c))
    for d in range(1, NX):
        signal(barrier, dev(up(x, d, NX), y, z, c))
    for d in range(1, NY):
        for e in range(2):
            signal(barrier, dev(x, up(y, d, NY), z, e))
    signal(barrier, sibling)
    for cp in loads:
        cp.wait()
    pl.semaphore_wait(barrier, 25)

    def wz_copy(n, d, zz):
        ref = wg.at[n, zz, x]
        return rcopy(ref, ref, s_wz.at[n, d - 1], r_wz.at[n, d - 1], dev(x, y, up(z, d, NZ), c))

    def wx_copy(n, d, zz, xx):
        ref = wg.at[n, zz, xx]
        return rcopy(ref, ref, s_wx.at[n, d - 1, zz], r_wx.at[n, d - 1, zz], dev(up(x, d, NX), y, z, c))

    def wx_start(n, zz):
        for d in (2, 1, 3):
            wx_copy(n, d, zz, x).start()

    def wz_start(n):
        for d in (4, 3, 5, 2, 6, 1, 7):
            wz_copy(n, d, z).start()

    def weights_forward(n):
        for d in (1, 7, 2, 6, 3, 5, 4):
            zz = down(z, d, NZ)
            wz_copy(n, d, zz).wait_recv()
            wx_start(n, zz)

    def weights_wait(n):
        for d in range(1, NX):
            for k in range(NZ):
                wx_copy(n, d, k, down(x, d, NX)).wait_recv()

    def row_copy(f, dr):
        to = dev(x, ynext, z, c) if dr == 0 else dev(x, yprev, z, c)
        return rcopy(xe.at[f, 2 + c], xe.at[f, 4 * dr + c], s_row.at[f, dr], r_row.at[f, dr], to)

    def fwd_copy(f, k, sending):
        core = c if sending else 1 - c
        ref = xe.at[f, 2 * k + core]
        return rcopy(ref, ref, s_fwd.at[f, k], r_fwd.at[f, k], sibling)

    wz_start(0)
    wx_start(0, z)
    for f in range(2):
        for dr in range(2):
            row_copy(f, dr).start()
        fwd_copy(f, 1, True).start()
        wz_start(1 + f)
    for n in (1, 2):
        wx_start(n, z)

    def rows_forward(f):
        for dr in range(2):
            row_copy(f, dr).wait_recv()
            fwd_copy(f, 2 * dr, True).start()

    def rows_wait(f):
        for k in range(3):
            fwd_copy(f, k, False).wait_recv()

    weights_forward(0)
    weights_forward(1)
    rows_forward(0)
    weights_forward(2)
    taps_in.wait()

    def gates_of(f):
        logits = lax.dot_general(
            xe[f, 1:5].reshape(640, 1024), bw_ref[...], (((1,), (1,)), ((), ())), preferred_element_type=F32
        )
        gates = jax.nn.sigmoid(logits)
        lanes = lax.broadcasted_iota(jnp.int32, (640, 8), 1)
        for s in range(2):
            picked = jnp.where(lanes == 4 * par + 2 * c + s, gates, 0.0)
            beta[f, s] = jnp.broadcast_to(jnp.sum(picked, axis=1, keepdims=True), (640, 128))

    rows_wait(0)
    gates_of(0)
    weights_wait(0)

    low = jnp.where(y == 0, 0.0, 1.0).astype(F32)
    high = jnp.where(y == NY - 1, 0.0, 1.0).astype(F32)

    def unit_owner(slot, f):
        j = 2 * c + slot
        return 2 * j + par, f

    ids = lax.broadcasted_iota(jnp.int32, (160, 128), 0)

    def project(f, n):
        proj[...] = (
            jnp.dot(
                xe[f].reshape(960, 1024), wg[n].reshape(1024, 256), preferred_element_type=F32
            )
            .astype(BF16)
            .reshape(6, 160, 256)
        )

    def stream(part_of, head, half, o):
        col = pl.multiple_of(part_of * 1024 + head * 128, 128)
        scale = {(0, 2): low, (1, 0): low, (2, 2): high, (3, 0): high}
        sums = [None] * 3
        for a in range(3):
            row = proj[o + a, :, half * 128 : (half + 1) * 128].astype(F32)
            for b in range(3):
                tap = ck_ref[a, pl.ds(b, 1), pl.ds(col, 128)]
                tap = tap * scale[(o, a)] if (o, a) in scale else tap
                sums[b] = row * tap if a == 0 else sums[b] + row * tap
        total = (
            jnp.where(ids > 0, pltpu.roll(sums[0], 1, 0), 0.0)
            + sums[1]
            + jnp.where(ids < 159, pltpu.roll(sums[2], 159, 0), 0.0)
        )
        return total * jax.nn.sigmoid(total)

    def normed(s):
        return (s * lax.rsqrt(jnp.sum(s * s, axis=-1, keepdims=True) + EPS)).astype(BF16)

    def step(i, carry):
        f, slot = lax.div(i, 2), lax.rem(i, 2)

        @pl.when(i == 1)
        def _():
            weights_wait(1)

        @pl.when(i == 2)
        def _():
            rows_forward(1)
            rows_wait(1)
            gates_of(1)

        project(f, slot)
        head = 4 * par + 2 * c + slot
        for o in range(4):
            here = slice(o * 160, (o + 1) * 160)
            key = normed(stream(1, head, 0, o))
            kv[here, :DK] = key
            wt[here, :] = (beta[f, slot, here, :] * key.astype(F32)).astype(BF16)
            kv[here, DK:] = stream(2, head, 1, o).astype(BF16)
        unit = lax.dot_general(
            wt[...], kv[...], (((0,), (0,)), ((), ())), preferred_element_type=F32
        ).astype(BF16)
        part[slot, f] = unit
        owner, core = unit_owner(slot, f)
        here = (owner == y) & (core == c)

        @pl.when(here)
        def _():
            got[half_y] = unit

        @pl.when(jnp.logical_not(here))
        def _():
            rcopy(
                part.at[slot, f], got.at[half_y], s_g.at[slot, f], r_g.at[half_y], dev(x, owner, z, core)
            ).start()

        return carry

    lax.fori_loop(0, 4, step, 0)

    weights_wait(2)

    def query(f, carry):
        project(f, 2)
        for slot in range(2):
            for o in range(4):
                qbuf[slot, o, f] = normed(stream(0, 4 * par + 2 * c + slot, slot, o))
        return carry

    lax.fori_loop(0, 2, query, 0)

    def q_out(slot, o, send):
        head = 4 * par + 2 * c + slot
        to = {0: dev(x, yprev, z, 1), 1: dev(x, y, z, 0), 2: dev(x, y, z, 1), 3: dev(x, ynext, z, 0)}[o]

        def far():
            cp = rcopy(qbuf.at[slot, o], q_ref.at[head], s_q.at[slot, o], r_q.at[head], to)
            cp.start() if send else cp.wait_send()

        if o in (0, 3):
            far()
            return
        pl.when(c != o - 1)(far)
        if send:

            @pl.when(c == o - 1)
            def _():
                pltpu.make_async_copy(qbuf.at[slot, o], q_ref.at[head], l_q.at[slot]).start()

    for slot in range(2):
        for o in (0, 3, 1, 2):
            q_out(slot, o, True)

    step_size = rate_ref[4 * par + half_y] * (DK / TOKENS)
    retain = jnp.exp(-jnp.full((DK, DK), decay_ref[c, 4 * par + half_y], F32))
    summed = None
    for k in range(4):
        source_is_here = (k == half_y) & (lax.div(half_y, 2) == c)

        @pl.when(jnp.logical_not(source_is_here))
        def _():
            rcopy(got.at[k], got.at[k], s_g.at[0, 0], r_g.at[k], sibling).wait_recv()

        summed = got[k].astype(F32) if summed is None else summed + got[k].astype(F32)
    gram, written = summed[:, :DK], summed[:, DK:]
    diagonal = lax.broadcasted_iota(jnp.int32, (DK, DK), 0) == lax.broadcasted_iota(
        jnp.int32, (DK, DK), 1
    )
    ident = jnp.where(diagonal, 1.0, 0.0)
    solved = inverse(ident + (0.5 * step_size) * (gram + gram.T), ident)
    own[:, :DK] = (retain * solved).astype(BF16)
    own[:, DK:] = (retain * close(solved, step_size * written)).astype(BF16)

    def compose(latter, earlier):
        both = jnp.dot(latter[:, :DK], earlier, preferred_element_type=F32)
        return jnp.concatenate([both[:, :DK], both[:, DK:] + latter[:, DK:].astype(F32)], axis=1).astype(BF16)

    pair = rcopy(own, fin, s_f, r_f, sibling)
    pair.start()
    pair.wait_recv()
    mine, other = own[...], fin[...]
    both = compose(jnp.where(c == 0, other, mine), jnp.where(c == 0, mine, other))
    px[x] = both

    def px_copy(d, xx):
        return rcopy(px.at[xx], px.at[xx], s_x.at[d - 1], r_x.at[d - 1], dev(up(x, d, NX), y, z, c))

    for d in (2, 1, 3):
        px_copy(d, x).start()
    for d in (1, 3, 2):
        px_copy(d, down(x, d, NX)).wait_recv()
    first = compose(px[1], px[0])
    line = compose(compose(px[3], px[2]), first)
    zin[0, z] = line[:, :DK]
    zin[1, z] = line[:, DK:]

    def z_copy(e):
        return rcopy(zin.at[c, z], zin.at[c, z], s_z.at[e - 1], r_z.at[z], dev(x, y, z + e, c))

    def zs_copy(k, sending):
        core = c if sending else 1 - c
        return rcopy(zin.at[core, k], zin.at[core, k], s_zs.at[k], r_zs.at[k], sibling)

    for e in range(NZ - 1, 0, -1):

        @pl.when(z + e < NZ)
        def _():
            z_copy(e).start()

    third = compose(px[2], first)
    current = jnp.where(c == 0, mine, both)
    before = jnp.where(x == 1, px[0], jnp.where(x == 2, first, third))
    fin[...] = jnp.where(x == 0, current, compose(current, before))

    for e in range(1, NZ):

        @pl.when(z >= e)
        def _():
            k = z - e
            rcopy(zin.at[c, k], zin.at[c, k], s_z.at[0], r_z.at[k], sibling).wait_recv()
            zs_copy(k, True).start()

    for k in range(NZ - 1):

        @pl.when(k < z)
        def _():
            zs_copy(k, False).wait_recv()
            if k == 0:
                state[...] = zin[1, 0].astype(F32)
            else:
                state[...] = jnp.dot(
                    zin[0, k], state[...].astype(BF16), preferred_element_type=F32
                ) + zin[1, k].astype(F32)

    @pl.when(z == 0)
    def _():
        cb[...] = fin[:, DK:]

    @pl.when(z > 0)
    def _():
        cb[...] = (
            jnp.dot(fin[:, :DK], state[...].astype(BF16), preferred_element_type=F32)
            + fin[:, DK:].astype(F32)
        ).astype(BF16)

    def sib_copy(k, sending):
        core = c if sending else 1 - c
        return rcopy(st.at[core, k], st.at[core, k], s_sib.at[k], r_sib.at[k], sibling)

    def st_copy(d, yy):
        return rcopy(cb, st.at[c, yy], s_st.at[d - 1], r_st.at[d - 1], dev(x, up(y, d, NY), z, c))

    for d in (4, 3, 5, 2, 6, 1, 7):
        st_copy(d, y).start()
    st[c, y] = cb[...]
    sib_copy(y, True).start()

    for slot in range(2):
        head = 4 * par + 2 * (1 - c) + slot
        rcopy(qbuf.at[slot, 0], q_ref.at[head], s_q.at[slot, 0], r_q.at[head], sibling).wait_recv()
        pltpu.make_async_copy(qbuf.at[slot, 0], q_ref.at[4 * par + 2 * c + slot], l_q.at[slot]).wait()
    for k in range(4):
        head = 4 * (1 - par) + k
        rcopy(qbuf.at[0, 0], q_ref.at[head], s_q.at[0, 0], r_q.at[head], sibling).wait_recv()

    def read(f, k):
        head = 4 * lax.rem(k, 2) + lax.div(k, 2)
        r = jnp.dot(q_ref[head, f], st[f, k], preferred_element_type=F32)
        r = r * lax.rsqrt(jnp.mean(r * r, axis=-1, keepdims=True) + EPS)
        lane = pl.ds(pl.multiple_of(head * DK, DK), DK)
        o_ref[f, 0, :, lane] = (r * gain_ref[:, lane]).astype(BF16)

    read(c, y)
    for d in (1, 7, 2, 6, 3, 5, 4):
        yy = down(y, d, NY)
        st_copy(d, yy).wait_recv()
        sib_copy(yy, True).start()
        read(c, yy)
    for d in (0, 1, 7, 2, 6, 3, 5, 4):
        yy = down(y, d, NY)
        sib_copy(yy, False).wait_recv()
        read(1 - c, yy)

    for slot in range(2):
        for o in range(4):
            q_out(slot, o, False)
    for slot in range(2):
        for f in range(2):
            owner, core = unit_owner(slot, f)

            @pl.when(jnp.logical_not((owner == y) & (core == c)))
            def _():
                rcopy(part.at[slot, f], got.at[0], s_g.at[slot, f], r_g.at[0], sibling).wait_send()

    for n in range(3):
        for d in range(1, NZ):
            wz_copy(n, d, z).wait_send()
        for d in range(1, NX):
            for k in range(NZ):
                wx_copy(n, d, k, x).wait_send()
    for d in range(1, NX):
        px_copy(d, x).wait_send()
    for f in range(2):
        for dr in range(2):
            row_copy(f, dr).wait_send()
        for k in range(3):
            fwd_copy(f, k, True).wait_send()
    pair.wait_send()
    for e in range(1, NZ):

        @pl.when(z + e < NZ)
        def _():
            z_copy(e).wait_send()

    for k in range(NZ - 1):

        @pl.when(k < z)
        def _():
            zs_copy(k, True).wait_send()

    for d in range(1, NY):
        st_copy(d, y).wait_send()
    for k in range(NY):
        sib_copy(k, True).wait_send()


def mix(latents, weight, beta_rows, conv_kernel, gain, step_rate, decay_rate):
    sem = pltpu.SemaphoreType.DMA
    return pl.pallas_call(
        mix_kernel,
        out_shape=jax.ShapeDtypeStruct((2, 1, 160, 1024), BF16),
        in_specs=[ANY, ANY, VM, ANY, VM, SM, SM],
        out_specs=VM,
        scratch_shapes=[
            pltpu.VMEM((2, 6, 160, 1024), BF16),
            pltpu.VMEM((3, NZ, NX, 32, 256), BF16),
            pltpu.VMEM((3, 3, 3072), F32),
            pltpu.VMEM((6, 160, 256), BF16),
            pltpu.VMEM((640, 256), BF16),
            pltpu.VMEM((640, DK), BF16),
            pltpu.VMEM((2, 2, 640, DK), F32),
            pltpu.VMEM((2, 4, 2, 160, DK), BF16),
            pltpu.VMEM((8, 2, 160, DK), BF16),
            pltpu.VMEM((2, 2, DK, 2 * DK), BF16),
            pltpu.VMEM((4, DK, 2 * DK), BF16),
            pltpu.VMEM((DK, 2 * DK), BF16),
            pltpu.VMEM((DK, 2 * DK), BF16),
            pltpu.VMEM((NX, DK, 2 * DK), BF16),
            pltpu.VMEM((2, NZ, DK, DK), BF16),
            pltpu.VMEM((DK, DK), F32),
            pltpu.VMEM((DK, DK), BF16),
            pltpu.VMEM((2, NY, DK, DK), BF16),
            sem((2, 2)), sem((2, 2)), sem((2, 3)), sem((2, 3)),
            sem((3, 7)), sem((3, 7)), sem((3, 3, 8)), sem((3, 3, 8)),
            sem((2, 2)), sem((4,)), sem((2, 4)), sem((8,)), sem((2,)), sem((9,)),
            sem(()), sem(()), sem((3,)), sem((3,)),
            sem((7,)), sem((8,)), sem((8,)), sem((8,)),
            sem((7,)), sem((7,)), sem((8,)), sem((8,)),
        ],
        compiler_params=pltpu.CompilerParams(
            collective_id=0, has_side_effects=True, vmem_limit_bytes=56 * 2**20
        ),
        name="mix",
    )(latents, weight, beta_rows, conv_kernel, gain, step_rate, decay_rate)


def body(video_latents, qkv_weight, beta_weight, conv_kernel, decay_rate, step_rate, output_gain):
    return mix(
        video_latents.reshape(2, 160, 1024), qkv_weight, beta_weight.T, conv_kernel,
        output_gain.reshape(1, 1024), step_rate, decay_rate,
    )


def solution(mesh):
    placed = (P("tm", "height", None, None), P("tm", None), P(), P(), P("tm", None), P(), P())
    return jax.shard_map(
        body, mesh=mesh, in_specs=placed, out_specs=P("tm", "height", None, None), check_vma=False
    )
```

```python
import functools

import jax
import jax.numpy as jnp
from jax import lax
from jax.experimental import pallas as pl
from jax.experimental.pallas import tpu as pltpu
from jax.sharding import PartitionSpec as P

MESH = pl.DeviceIdType.MESH
EPS = 1e-06
F32 = jnp.float32
BF16 = jnp.bfloat16
NX, NZ, NY = 4, 8, 8
TOKENS = 64 * 16 * 160
DK = 128
VM = pl.BlockSpec(memory_space=pltpu.VMEM)
SM = pl.BlockSpec(memory_space=pltpu.SMEM)
ANY = pl.BlockSpec(memory_space=pl.ANY)


def place():
    t, h = lax.axis_index("tm"), lax.axis_index("height")
    return lax.rem(t, NX), lax.div(h, 2), lax.div(t, NX), lax.rem(h, 2)


def dev(x, y, z, c):
    return (z * NX + x, y * 2 + c)


def up(i, d, n):
    return lax.rem(i + d, n)


def down(i, d, n):
    return lax.rem(i + n - d, n)


def rcopy(src, dst, ssem, rsem, to):
    return pltpu.make_async_remote_copy(
        src_ref=src, dst_ref=dst, send_sem=ssem, recv_sem=rsem, device_id=to, device_id_type=MESH
    )


def signal(barrier, to):
    pl.semaphore_signal(barrier, inc=1, device_id=to, device_id_type=MESH)


def halves(a):
    high = a.astype(BF16)
    return high, (a - high.astype(F32)).astype(BF16)


def close(a, b):
    a_high, a_low = halves(a)
    b_high, b_low = halves(b)
    both = jnp.concatenate([a_high, a_low], axis=1)
    return jnp.dot(
        both, jnp.concatenate([b_high, b_high], axis=0), preferred_element_type=F32
    ) + jnp.dot(a_high, b_low, preferred_element_type=F32)


def inverse(system, ident):
    power = ident - 0.4 * system
    total = ident + power
    power = close(power, power)
    for _ in range(3):
        stacked = close(jnp.concatenate([power, total], axis=0), power)
        power, total = stacked[:DK], total + stacked[DK:]
    return 0.4 * (total + close(total, power))


def mix_kernel(
    x_ref, w_ref, bw_ref, ck_hbm, gain_ref, rate_ref, decay_ref, o_ref,
    xe, wg, ck_ref, proj, kv, wt, beta, qbuf, q_ref, part, got, own, fin, px, zin, state, cb, st,
    s_row, r_row, s_fwd, r_fwd, s_wz, r_wz, s_wx, r_wx, s_g, r_g, s_q, r_q, l_q, l_in,
    s_f, r_f, s_x, r_x, s_z, r_z, s_zs, r_zs, s_st, r_st, s_sib, r_sib,
):
    x, y, z, c = place()
    par, half_y = lax.rem(y, 2), lax.div(y, 2)
    sibling = dev(x, y, z, 1 - c)
    ynext, yprev = up(y, 1, NY), down(y, 1, NY)

    loads = [pltpu.make_async_copy(x_ref.at[f], xe.at[f, 2 + c], l_in.at[f]) for f in range(2)]
    for s in range(2):
        for g in range(3):
            col = pl.multiple_of(g * 1024 + (4 * par + 2 * c + s) * 128, 128)
            block, lane = (2, s * 128) if g == 0 else (s, (g - 1) * 128)
            loads.append(
                pltpu.make_async_copy(
                    w_ref.at[:, pl.ds(col, 128)], wg.at[block, z, x, :, pl.ds(lane, 128)], l_in.at[2 + 3 * s + g]
                )
            )
    taps_in = pltpu.make_async_copy(ck_hbm, ck_ref, l_in.at[8])
    for cp in loads:
        cp.start()
    taps_in.start()

    barrier = pltpu.get_barrier_semaphore()
    for d in range(1, NZ):
        signal(barrier, dev(x, y, up(z, d, NZ), c))
    for d in range(1, NX):
        signal(barrier, dev(up(x, d, NX), y, z, c))
    for d in range(1, NY):
        for e in range(2):
            signal(barrier, dev(x, up(y, d, NY), z, e))
    signal(barrier, sibling)
    for cp in loads:
        cp.wait()
    pl.semaphore_wait(barrier, 25)

    def wz_copy(n, d, zz):
        ref = wg.at[n, zz, x]
        return rcopy(ref, ref, s_wz.at[n, d - 1], r_wz.at[n, d - 1], dev(x, y, up(z, d, NZ), c))

    def wx_copy(n, d, zz, xx):
        ref = wg.at[n, zz, xx]
        return rcopy(ref, ref, s_wx.at[n, d - 1, zz], r_wx.at[n, d - 1, zz], dev(up(x, d, NX), y, z, c))

    def wx_start(n, zz):
        for d in (2, 1, 3):
            wx_copy(n, d, zz, x).start()

    def wz_start(n):
        for d in (1, 7, 2, 6, 3, 5, 4):
            wz_copy(n, d, z).start()

    def weights_forward(n):
        for d in (1, 7, 2, 6, 3, 5, 4):
            zz = down(z, d, NZ)
            wz_copy(n, d, zz).wait_recv()
            wx_start(n, zz)

    def weights_wait(n):
        for d in range(1, NX):
            for k in range(NZ):
                wx_copy(n, d, k, down(x, d, NX)).wait_recv()

    def row_copy(f, dr, hf):
        to = dev(x, ynext, z, c) if dr == 0 else dev(x, yprev, z, c)
        cols = pl.ds(80 * hf, 80)
        return rcopy(
            xe.at[f, 2 + c, cols], xe.at[f, 4 * dr + c, cols], s_row.at[f, dr, hf], r_row.at[f, dr, hf], to
        )

    def fwd_copy(f, k, hf, sending):
        core = c if sending else 1 - c
        ref = xe.at[f, 2 * k + core, pl.ds(80 * hf, 80)]
        return rcopy(ref, ref, s_fwd.at[f, k, hf], r_fwd.at[f, k, hf], sibling)

    wz_start(0)
    wx_start(0, z)
    for f in range(2):
        for hf in range(2):
            for dr in range(2):
                row_copy(f, dr, hf).start()
        for hf in range(2):
            fwd_copy(f, 1, hf, True).start()
        if f == 0:
            wz_start(1)
            wx_start(1, z)

    def rows_forward(f):
        for hf in range(2):
            for dr in range(2):
                row_copy(f, dr, hf).wait_recv()
                fwd_copy(f, 2 * dr, hf, True).start()

    def rows_wait(f):
        for k in range(3):
            for hf in range(2):
                fwd_copy(f, k, hf, False).wait_recv()

    weights_forward(0)
    wz_start(2)
    weights_forward(1)
    wx_start(2, z)
    rows_forward(0)
    taps_in.wait()

    def gates_of(f):
        logits = lax.dot_general(
            xe[f, 1:5].reshape(640, 1024), bw_ref[...], (((1,), (1,)), ((), ())), preferred_element_type=F32
        )
        gates = jax.nn.sigmoid(logits)
        lanes = lax.broadcasted_iota(jnp.int32, (640, 8), 1)
        for s in range(2):
            picked = jnp.where(lanes == 4 * par + 2 * c + s, gates, 0.0)
            beta[f, s] = jnp.broadcast_to(jnp.sum(picked, axis=1, keepdims=True), (640, 128))

    rows_wait(0)
    gates_of(0)
    weights_wait(0)

    low = jnp.where(y == 0, 0.0, 1.0).astype(F32)
    high = jnp.where(y == NY - 1, 0.0, 1.0).astype(F32)

    def unit_owner(slot, f):
        j = 2 * c + slot
        return 2 * j + par, f

    ids = lax.broadcasted_iota(jnp.int32, (160, 128), 0)

    def project(f, n):
        proj[...] = (
            jnp.dot(
                xe[f].reshape(960, 1024), wg[n].reshape(1024, 256), preferred_element_type=F32
            )
            .astype(BF16)
            .reshape(6, 160, 256)
        )

    def stream(part_of, head, half, o):
        col = pl.multiple_of(part_of * 1024 + head * 128, 128)
        scale = {(0, 2): low, (1, 0): low, (2, 2): high, (3, 0): high}
        sums = [None] * 3
        for a in range(3):
            row = proj[o + a, :, half * 128 : (half + 1) * 128].astype(F32)
            for b in range(3):
                tap = ck_ref[a, pl.ds(b, 1), pl.ds(col, 128)]
                tap = tap * scale[(o, a)] if (o, a) in scale else tap
                sums[b] = row * tap if a == 0 else sums[b] + row * tap
        total = (
            jnp.where(ids > 0, pltpu.roll(sums[0], 1, 0), 0.0)
            + sums[1]
            + jnp.where(ids < 159, pltpu.roll(sums[2], 159, 0), 0.0)
        )
        return total * jax.nn.sigmoid(total)

    def normed(s):
        return (s * lax.rsqrt(jnp.sum(s * s, axis=-1, keepdims=True) + EPS)).astype(BF16)

    def step(i, carry):
        slot, f = lax.div(i, 2), lax.rem(i, 2)

        @pl.when(i == 1)
        def _():
            weights_forward(2)
            rows_forward(1)
            rows_wait(1)
            gates_of(1)

        @pl.when(i == 2)
        def _():
            weights_wait(1)

        project(f, slot)
        head = 4 * par + 2 * c + slot
        for o in range(4):
            here = slice(o * 160, (o + 1) * 160)
            key = normed(stream(1, head, 0, o))
            kv[here, :DK] = key
            wt[here, :] = (beta[f, slot, here, :] * key.astype(F32)).astype(BF16)
            kv[here, DK:] = stream(2, head, 1, o).astype(BF16)
        unit = lax.dot_general(
            wt[...], kv[...], (((0,), (0,)), ((), ())), preferred_element_type=F32
        ).astype(BF16)
        part[slot, f] = unit
        owner, core = unit_owner(slot, f)
        here = (owner == y) & (core == c)

        @pl.when(here)
        def _():
            got[half_y] = unit

        @pl.when(jnp.logical_not(here))
        def _():
            rcopy(
                part.at[slot, f], got.at[half_y], s_g.at[slot, f], r_g.at[half_y], dev(x, owner, z, core)
            ).start()

        return carry

    lax.fori_loop(0, 4, step, 0)

    weights_wait(2)

    def query(f, carry):
        project(f, 2)
        for slot in range(2):
            for o in range(4):
                qbuf[slot, o, f] = normed(stream(0, 4 * par + 2 * c + slot, slot, o))
        return carry

    lax.fori_loop(0, 2, query, 0)

    def q_out(slot, o, send):
        head = 4 * par + 2 * c + slot
        to = {0: dev(x, yprev, z, 1), 1: dev(x, y, z, 0), 2: dev(x, y, z, 1), 3: dev(x, ynext, z, 0)}[o]

        def far():
            cp = rcopy(qbuf.at[slot, o], q_ref.at[head], s_q.at[slot, o], r_q.at[head], to)
            cp.start() if send else cp.wait_send()

        if o in (0, 3):
            far()
            return
        pl.when(c != o - 1)(far)
        if send:

            @pl.when(c == o - 1)
            def _():
                pltpu.make_async_copy(qbuf.at[slot, o], q_ref.at[head], l_q.at[slot]).start()

    for slot in range(2):
        for o in (0, 3, 1, 2):
            q_out(slot, o, True)

    step_size = rate_ref[4 * par + half_y] * (DK / TOKENS)
    retain = jnp.exp(-jnp.full((DK, DK), decay_ref[c, 4 * par + half_y], F32))
    summed = None
    for k in range(4):
        source_is_here = (k == half_y) & (lax.div(half_y, 2) == c)

        @pl.when(jnp.logical_not(source_is_here))
        def _():
            rcopy(got.at[k], got.at[k], s_g.at[0, 0], r_g.at[k], sibling).wait_recv()

        summed = got[k].astype(F32) if summed is None else summed + got[k].astype(F32)
    gram, written = summed[:, :DK], summed[:, DK:]
    diagonal = lax.broadcasted_iota(jnp.int32, (DK, DK), 0) == lax.broadcasted_iota(
        jnp.int32, (DK, DK), 1
    )
    ident = jnp.where(diagonal, 1.0, 0.0)
    solved = inverse(ident + (0.5 * step_size) * (gram + gram.T), ident)
    own[:, :DK] = (retain * solved).astype(BF16)
    own[:, DK:] = (retain * close(solved, step_size * written)).astype(BF16)

    def compose(latter, earlier):
        both = jnp.dot(latter[:, :DK], earlier, preferred_element_type=F32)
        return jnp.concatenate([both[:, :DK], both[:, DK:] + latter[:, DK:].astype(F32)], axis=1).astype(BF16)

    pair = rcopy(own, fin, s_f, r_f, sibling)
    pair.start()
    pair.wait_recv()
    mine, other = own[...], fin[...]
    both = compose(jnp.where(c == 0, other, mine), jnp.where(c == 0, mine, other))
    px[x] = both

    def px_copy(d, xx):
        return rcopy(px.at[xx], px.at[xx], s_x.at[d - 1], r_x.at[d - 1], dev(up(x, d, NX), y, z, c))

    for d in (2, 1, 3):
        px_copy(d, x).start()
    for d in (1, 3, 2):
        px_copy(d, down(x, d, NX)).wait_recv()
    first = compose(px[1], px[0])
    line = compose(compose(px[3], px[2]), first)
    zin[0, z] = line[:, :DK]
    zin[1, z] = line[:, DK:]

    def z_copy(e):
        return rcopy(zin.at[c, z], zin.at[c, z], s_z.at[e - 1], r_z.at[z], dev(x, y, z + e, c))

    def zs_copy(k, sending):
        core = c if sending else 1 - c
        return rcopy(zin.at[core, k], zin.at[core, k], s_zs.at[k], r_zs.at[k], sibling)

    for e in range(NZ - 1, 0, -1):

        @pl.when(z + e < NZ)
        def _():
            z_copy(e).start()

    third = compose(px[2], first)
    current = jnp.where(c == 0, mine, both)
    before = jnp.where(x == 1, px[0], jnp.where(x == 2, first, third))
    fin[...] = jnp.where(x == 0, current, compose(current, before))

    for e in range(1, NZ):

        @pl.when(z >= e)
        def _():
            k = z - e
            rcopy(zin.at[c, k], zin.at[c, k], s_z.at[0], r_z.at[k], sibling).wait_recv()
            zs_copy(k, True).start()

    for k in range(NZ - 1):

        @pl.when(k < z)
        def _():
            zs_copy(k, False).wait_recv()
            if k == 0:
                state[...] = zin[1, 0].astype(F32)
            else:
                state[...] = jnp.dot(
                    zin[0, k], state[...].astype(BF16), preferred_element_type=F32
                ) + zin[1, k].astype(F32)

    @pl.when(z == 0)
    def _():
        cb[...] = fin[:, DK:]

    @pl.when(z > 0)
    def _():
        cb[...] = (
            jnp.dot(fin[:, :DK], state[...].astype(BF16), preferred_element_type=F32)
            + fin[:, DK:].astype(F32)
        ).astype(BF16)

    def sib_copy(k, sending):
        core = c if sending else 1 - c
        return rcopy(st.at[core, k], st.at[core, k], s_sib.at[k], r_sib.at[k], sibling)

    def st_copy(d, yy):
        return rcopy(cb, st.at[c, yy], s_st.at[d - 1], r_st.at[d - 1], dev(x, up(y, d, NY), z, c))

    for d in (4, 3, 5, 2, 6, 1, 7):
        st_copy(d, y).start()
    st[c, y] = cb[...]
    sib_copy(y, True).start()

    for slot in range(2):
        head = 4 * par + 2 * (1 - c) + slot
        rcopy(qbuf.at[slot, 0], q_ref.at[head], s_q.at[slot, 0], r_q.at[head], sibling).wait_recv()
        pltpu.make_async_copy(qbuf.at[slot, 0], q_ref.at[4 * par + 2 * c + slot], l_q.at[slot]).wait()
    for k in range(4):
        head = 4 * (1 - par) + k
        rcopy(qbuf.at[0, 0], q_ref.at[head], s_q.at[0, 0], r_q.at[head], sibling).wait_recv()

    def read(f, k):
        head = 4 * lax.rem(k, 2) + lax.div(k, 2)
        r = jnp.dot(q_ref[head, f], st[f, k], preferred_element_type=F32)
        r = r * lax.rsqrt(jnp.mean(r * r, axis=-1, keepdims=True) + EPS)
        lane = pl.ds(pl.multiple_of(head * DK, DK), DK)
        o_ref[f, 0, :, lane] = (r * gain_ref[:, lane]).astype(BF16)

    read(c, y)
    for d in (1, 7, 2, 6, 3, 5, 4):
        yy = down(y, d, NY)
        st_copy(d, yy).wait_recv()
        sib_copy(yy, True).start()
        read(c, yy)
    for d in (0, 1, 7, 2, 6, 3, 5, 4):
        yy = down(y, d, NY)
        sib_copy(yy, False).wait_recv()
        read(1 - c, yy)

    for slot in range(2):
        for o in range(4):
            q_out(slot, o, False)
    for slot in range(2):
        for f in range(2):
            owner, core = unit_owner(slot, f)

            @pl.when(jnp.logical_not((owner == y) & (core == c)))
            def _():
                rcopy(part.at[slot, f], got.at[0], s_g.at[slot, f], r_g.at[0], sibling).wait_send()

    for n in range(3):
        for d in range(1, NZ):
            wz_copy(n, d, z).wait_send()
        for d in range(1, NX):
            for k in range(NZ):
                wx_copy(n, d, k, x).wait_send()
    for d in range(1, NX):
        px_copy(d, x).wait_send()
    for f in range(2):
        for hf in range(2):
            for dr in range(2):
                row_copy(f, dr, hf).wait_send()
            for k in range(3):
                fwd_copy(f, k, hf, True).wait_send()
    pair.wait_send()
    for e in range(1, NZ):

        @pl.when(z + e < NZ)
        def _():
            z_copy(e).wait_send()

    for k in range(NZ - 1):

        @pl.when(k < z)
        def _():
            zs_copy(k, True).wait_send()

    for d in range(1, NY):
        st_copy(d, y).wait_send()
    for k in range(NY):
        sib_copy(k, True).wait_send()


def mix(latents, weight, beta_rows, conv_kernel, gain, step_rate, decay_rate):
    sem = pltpu.SemaphoreType.DMA
    return pl.pallas_call(
        mix_kernel,
        out_shape=jax.ShapeDtypeStruct((2, 1, 160, 1024), BF16),
        in_specs=[ANY, ANY, VM, ANY, VM, SM, SM],
        out_specs=VM,
        scratch_shapes=[
            pltpu.VMEM((2, 6, 160, 1024), BF16),
            pltpu.VMEM((3, NZ, NX, 32, 256), BF16),
            pltpu.VMEM((3, 3, 3072), F32),
            pltpu.VMEM((6, 160, 256), BF16),
            pltpu.VMEM((640, 256), BF16),
            pltpu.VMEM((640, DK), BF16),
            pltpu.VMEM((2, 2, 640, DK), F32),
            pltpu.VMEM((2, 4, 2, 160, DK), BF16),
            pltpu.VMEM((8, 2, 160, DK), BF16),
            pltpu.VMEM((2, 2, DK, 2 * DK), BF16),
            pltpu.VMEM((4, DK, 2 * DK), BF16),
            pltpu.VMEM((DK, 2 * DK), BF16),
            pltpu.VMEM((DK, 2 * DK), BF16),
            pltpu.VMEM((NX, DK, 2 * DK), BF16),
            pltpu.VMEM((2, NZ, DK, DK), BF16),
            pltpu.VMEM((DK, DK), F32),
            pltpu.VMEM((DK, DK), BF16),
            pltpu.VMEM((2, NY, DK, DK), BF16),
            sem((2, 2, 2)), sem((2, 2, 2)), sem((2, 3, 2)), sem((2, 3, 2)),
            sem((3, 7)), sem((3, 7)), sem((3, 3, 8)), sem((3, 3, 8)),
            sem((2, 2)), sem((4,)), sem((2, 4)), sem((8,)), sem((2,)), sem((9,)),
            sem(()), sem(()), sem((3,)), sem((3,)),
            sem((7,)), sem((8,)), sem((8,)), sem((8,)),
            sem((7,)), sem((7,)), sem((8,)), sem((8,)),
        ],
        compiler_params=pltpu.CompilerParams(
            collective_id=0, has_side_effects=True, vmem_limit_bytes=56 * 2**20
        ),
        name="mix",
    )(latents, weight, beta_rows, conv_kernel, gain, step_rate, decay_rate)


def body(video_latents, qkv_weight, beta_weight, conv_kernel, decay_rate, step_rate, output_gain):
    return mix(
        video_latents.reshape(2, 160, 1024), qkv_weight, beta_weight.T, conv_kernel,
        output_gain.reshape(1, 1024), step_rate, decay_rate,
    )


def solution(mesh):
    placed = (P("tm", "height", None, None), P("tm", None), P(), P(), P("tm", None), P(), P())
    return jax.shard_map(
        body, mesh=mesh, in_specs=placed, out_specs=P("tm", "height", None, None), check_vma=False
    )
```

```python
import functools

import jax
import jax.numpy as jnp
from jax import lax
from jax.experimental import pallas as pl
from jax.experimental.pallas import tpu as pltpu
from jax.sharding import PartitionSpec as P

MESH = pl.DeviceIdType.MESH
EPS = 1e-06
F32 = jnp.float32
BF16 = jnp.bfloat16
NX, NZ, NY = 4, 8, 8
TOKENS = 64 * 16 * 160
DK = 128
VM = pl.BlockSpec(memory_space=pltpu.VMEM)
SM = pl.BlockSpec(memory_space=pltpu.SMEM)
ANY = pl.BlockSpec(memory_space=pl.ANY)


def place():
    t, h = lax.axis_index("tm"), lax.axis_index("height")
    return lax.rem(t, NX), lax.div(h, 2), lax.div(t, NX), lax.rem(h, 2)


def dev(x, y, z, c):
    return (z * NX + x, y * 2 + c)


def up(i, d, n):
    return lax.rem(i + d, n)


def down(i, d, n):
    return lax.rem(i + n - d, n)


def rcopy(src, dst, ssem, rsem, to):
    return pltpu.make_async_remote_copy(
        src_ref=src, dst_ref=dst, send_sem=ssem, recv_sem=rsem, device_id=to, device_id_type=MESH
    )


def signal(barrier, to):
    pl.semaphore_signal(barrier, inc=1, device_id=to, device_id_type=MESH)


def halves(a):
    high = a.astype(BF16)
    return high, (a - high.astype(F32)).astype(BF16)


def close(a, b):
    a_high, a_low = halves(a)
    b_high, b_low = halves(b)
    both = jnp.concatenate([a_high, a_low], axis=1)
    return jnp.dot(
        both, jnp.concatenate([b_high, b_high], axis=0), preferred_element_type=F32
    ) + jnp.dot(a_high, b_low, preferred_element_type=F32)


def inverse(system, ident):
    power = ident - 0.4 * system
    total = ident + power
    power = close(power, power)
    for _ in range(3):
        stacked = close(jnp.concatenate([power, total], axis=0), power)
        power, total = stacked[:DK], total + stacked[DK:]
    return 0.4 * (total + close(total, power))


def mix_kernel(
    x_ref, w_ref, bw_ref, ck_hbm, gain_ref, rate_ref, decay_ref, o_ref,
    xe, wg, ck_ref, proj, kv, wt, beta, qbuf, q_ref, part, got, own, fin, px, zin, state, cb, st,
    s_row, r_row, s_fwd, r_fwd, s_wz, r_wz, s_wx, r_wx, s_g, r_g, s_q, r_q, l_q, l_in,
    s_f, r_f, s_x, r_x, s_z, r_z, s_zs, r_zs, s_st, r_st, s_sib, r_sib,
):
    x, y, z, c = place()
    par, half_y = lax.rem(y, 2), lax.div(y, 2)
    sibling = dev(x, y, z, 1 - c)
    ynext, yprev = up(y, 1, NY), down(y, 1, NY)

    loads = [pltpu.make_async_copy(x_ref.at[f], xe.at[f, 2 + c], l_in.at[f]) for f in range(2)]
    for s in range(2):
        for g in range(3):
            col = pl.multiple_of(g * 1024 + (4 * par + 2 * c + s) * 128, 128)
            block, lane = (2, s * 128) if g == 0 else (s, (g - 1) * 128)
            loads.append(
                pltpu.make_async_copy(
                    w_ref.at[:, pl.ds(col, 128)], wg.at[block, z, x, :, pl.ds(lane, 128)], l_in.at[2 + 3 * s + g]
                )
            )
    taps_in = pltpu.make_async_copy(ck_hbm, ck_ref, l_in.at[8])
    for cp in loads:
        cp.start()
    taps_in.start()

    barrier = pltpu.get_barrier_semaphore()
    for d in range(1, NZ):
        signal(barrier, dev(x, y, up(z, d, NZ), c))
    for d in range(1, NX):
        signal(barrier, dev(up(x, d, NX), y, z, c))
    for d in range(1, NY):
        for e in range(2):
            signal(barrier, dev(x, up(y, d, NY), z, e))
    signal(barrier, sibling)
    for cp in loads:
        cp.wait()
    pl.semaphore_wait(barrier, 25)

    def wz_copy(n, d, zz):
        ref = wg.at[n, zz, x]
        return rcopy(ref, ref, s_wz.at[n, d - 1], r_wz.at[n, d - 1], dev(x, y, up(z, d, NZ), c))

    def wx_copy(n, d, zz, xx):
        ref = wg.at[n, zz, xx]
        return rcopy(ref, ref, s_wx.at[n, d - 1, zz], r_wx.at[n, d - 1, zz], dev(up(x, d, NX), y, z, c))

    def wx_start(n, zz):
        for d in (2, 1, 3):
            wx_copy(n, d, zz, x).start()

    def wz_start(n):
        for d in (1, 7, 2, 6, 3, 5, 4):
            wz_copy(n, d, z).start()

    def weights_forward(n):
        for d in (1, 7, 2, 6, 3, 5, 4):
            zz = down(z, d, NZ)
            wz_copy(n, d, zz).wait_recv()
            wx_start(n, zz)

    def weights_wait(n):
        for d in range(1, NX):
            for k in range(NZ):
                wx_copy(n, d, k, down(x, d, NX)).wait_recv()

    def row_copy(f, dr, hf):
        to = dev(x, ynext, z, c) if dr == 0 else dev(x, yprev, z, c)
        cols = pl.ds(80 * hf, 80)
        return rcopy(
            xe.at[f, 2 + c, cols], xe.at[f, 4 * dr + c, cols], s_row.at[f, dr, hf], r_row.at[f, dr, hf], to
        )

    def fwd_copy(f, k, hf, sending):
        core = c if sending else 1 - c
        ref = xe.at[f, 2 * k + core, pl.ds(80 * hf, 80)]
        return rcopy(ref, ref, s_fwd.at[f, k, hf], r_fwd.at[f, k, hf], sibling)

    wz_start(0)
    wx_start(0, z)
    for f in range(2):
        for hf in range(2):
            for dr in range(2):
                row_copy(f, dr, hf).start()
        for hf in range(2):
            fwd_copy(f, 1, hf, True).start()
        if f == 0:
            wz_start(1)
            wx_start(1, z)

    def rows_forward(f):
        for hf in range(2):
            for dr in range(2):
                row_copy(f, dr, hf).wait_recv()
                fwd_copy(f, 2 * dr, hf, True).start()

    def rows_wait(f):
        for k in range(3):
            for hf in range(2):
                fwd_copy(f, k, hf, False).wait_recv()

    weights_forward(0)
    weights_forward(1)
    wz_start(2)
    rows_forward(0)
    wx_start(2, z)
    taps_in.wait()

    def gates_of(f):
        logits = lax.dot_general(
            xe[f, 1:5].reshape(640, 1024), bw_ref[...], (((1,), (1,)), ((), ())), preferred_element_type=F32
        )
        gates = jax.nn.sigmoid(logits)
        lanes = lax.broadcasted_iota(jnp.int32, (640, 8), 1)
        for s in range(2):
            picked = jnp.where(lanes == 4 * par + 2 * c + s, gates, 0.0)
            beta[f, s] = jnp.broadcast_to(jnp.sum(picked, axis=1, keepdims=True), (640, 128))

    rows_wait(0)
    gates_of(0)
    weights_wait(0)

    low = jnp.where(y == 0, 0.0, 1.0).astype(F32)
    high = jnp.where(y == NY - 1, 0.0, 1.0).astype(F32)

    def unit_owner(slot, f):
        j = 2 * c + slot
        return 2 * j + par, f

    ids = lax.broadcasted_iota(jnp.int32, (160, 128), 0)

    def project(f, n):
        proj[...] = (
            jnp.dot(
                xe[f].reshape(960, 1024), wg[n].reshape(1024, 256), preferred_element_type=F32
            )
            .astype(BF16)
            .reshape(6, 160, 256)
        )

    def stream(part_of, head, half, o):
        col = pl.multiple_of(part_of * 1024 + head * 128, 128)
        scale = {(0, 2): low, (1, 0): low, (2, 2): high, (3, 0): high}
        sums = [None] * 3
        for a in range(3):
            row = proj[o + a, :, half * 128 : (half + 1) * 128].astype(F32)
            for b in range(3):
                tap = ck_ref[a, pl.ds(b, 1), pl.ds(col, 128)]
                tap = tap * scale[(o, a)] if (o, a) in scale else tap
                sums[b] = row * tap if a == 0 else sums[b] + row * tap
        total = (
            jnp.where(ids > 0, pltpu.roll(sums[0], 1, 0), 0.0)
            + sums[1]
            + jnp.where(ids < 159, pltpu.roll(sums[2], 159, 0), 0.0)
        )
        return total * jax.nn.sigmoid(total)

    def normed(s):
        return (s * lax.rsqrt(jnp.sum(s * s, axis=-1, keepdims=True) + EPS)).astype(BF16)

    def step(i, carry):
        f, slot = lax.div(i, 2), lax.rem(i, 2)

        @pl.when(i == 1)
        def _():
            weights_forward(2)
            rows_forward(1)
            weights_wait(1)

        @pl.when(i == 2)
        def _():
            rows_wait(1)
            gates_of(1)

        project(f, slot)
        head = 4 * par + 2 * c + slot
        for o in range(4):
            here = slice(o * 160, (o + 1) * 160)
            key = normed(stream(1, head, 0, o))
            kv[here, :DK] = key
            wt[here, :] = (beta[f, slot, here, :] * key.astype(F32)).astype(BF16)
            kv[here, DK:] = stream(2, head, 1, o).astype(BF16)
        unit = lax.dot_general(
            wt[...], kv[...], (((0,), (0,)), ((), ())), preferred_element_type=F32
        ).astype(BF16)
        part[slot, f] = unit
        owner, core = unit_owner(slot, f)
        here = (owner == y) & (core == c)

        @pl.when(here)
        def _():
            got[half_y] = unit

        @pl.when(jnp.logical_not(here))
        def _():
            rcopy(
                part.at[slot, f], got.at[half_y], s_g.at[slot, f], r_g.at[half_y], dev(x, owner, z, core)
            ).start()

        return carry

    lax.fori_loop(0, 4, step, 0)

    weights_wait(2)

    def query(f, carry):
        project(f, 2)
        for slot in range(2):
            for o in range(4):
                qbuf[slot, o, f] = normed(stream(0, 4 * par + 2 * c + slot, slot, o))
        return carry

    lax.fori_loop(0, 2, query, 0)

    def q_out(slot, o, send):
        head = 4 * par + 2 * c + slot
        to = {0: dev(x, yprev, z, 1), 1: dev(x, y, z, 0), 2: dev(x, y, z, 1), 3: dev(x, ynext, z, 0)}[o]

        def far():
            cp = rcopy(qbuf.at[slot, o], q_ref.at[head], s_q.at[slot, o], r_q.at[head], to)
            cp.start() if send else cp.wait_send()

        if o in (0, 3):
            far()
            return
        pl.when(c != o - 1)(far)
        if send:

            @pl.when(c == o - 1)
            def _():
                pltpu.make_async_copy(qbuf.at[slot, o], q_ref.at[head], l_q.at[slot]).start()

    for slot in range(2):
        for o in (0, 3, 1, 2):
            q_out(slot, o, True)

    step_size = rate_ref[4 * par + half_y] * (DK / TOKENS)
    retain = jnp.exp(-jnp.full((DK, DK), decay_ref[c, 4 * par + half_y], F32))
    summed = None
    for k in range(4):
        source_is_here = (k == half_y) & (lax.div(half_y, 2) == c)

        @pl.when(jnp.logical_not(source_is_here))
        def _():
            rcopy(got.at[k], got.at[k], s_g.at[0, 0], r_g.at[k], sibling).wait_recv()

        summed = got[k].astype(F32) if summed is None else summed + got[k].astype(F32)
    gram, written = summed[:, :DK], summed[:, DK:]
    diagonal = lax.broadcasted_iota(jnp.int32, (DK, DK), 0) == lax.broadcasted_iota(
        jnp.int32, (DK, DK), 1
    )
    ident = jnp.where(diagonal, 1.0, 0.0)
    solved = inverse(ident + (0.5 * step_size) * (gram + gram.T), ident)
    own[:, :DK] = (retain * solved).astype(BF16)
    own[:, DK:] = (retain * close(solved, step_size * written)).astype(BF16)

    def compose(latter, earlier):
        both = jnp.dot(latter[:, :DK], earlier, preferred_element_type=F32)
        return jnp.concatenate([both[:, :DK], both[:, DK:] + latter[:, DK:].astype(F32)], axis=1).astype(BF16)

    pair = rcopy(own, fin, s_f, r_f, sibling)
    pair.start()
    pair.wait_recv()
    mine, other = own[...], fin[...]
    both = compose(jnp.where(c == 0, other, mine), jnp.where(c == 0, mine, other))
    px[x] = both

    def px_copy(d, xx):
        return rcopy(px.at[xx], px.at[xx], s_x.at[d - 1], r_x.at[d - 1], dev(up(x, d, NX), y, z, c))

    for d in (2, 1, 3):
        px_copy(d, x).start()
    for d in (1, 3, 2):
        px_copy(d, down(x, d, NX)).wait_recv()
    first = compose(px[1], px[0])
    line = compose(compose(px[3], px[2]), first)
    zin[0, z] = line[:, :DK]
    zin[1, z] = line[:, DK:]

    def z_copy(e):
        return rcopy(zin.at[c, z], zin.at[c, z], s_z.at[e - 1], r_z.at[z], dev(x, y, z + e, c))

    def zs_copy(k, sending):
        core = c if sending else 1 - c
        return rcopy(zin.at[core, k], zin.at[core, k], s_zs.at[k], r_zs.at[k], sibling)

    for e in range(1, NZ):

        @pl.when(z + e < NZ)
        def _():
            z_copy(e).start()

    third = compose(px[2], first)
    current = jnp.where(c == 0, mine, both)
    before = jnp.where(x == 1, px[0], jnp.where(x == 2, first, third))
    fin[...] = jnp.where(x == 0, current, compose(current, before))

    for e in range(1, NZ):

        @pl.when(z >= e)
        def _():
            k = z - e
            rcopy(zin.at[c, k], zin.at[c, k], s_z.at[0], r_z.at[k], sibling).wait_recv()
            zs_copy(k, True).start()

    for k in range(NZ - 1):

        @pl.when(k < z)
        def _():
            zs_copy(k, False).wait_recv()
            if k == 0:
                state[...] = zin[1, 0].astype(F32)
            else:
                state[...] = jnp.dot(
                    zin[0, k], state[...].astype(BF16), preferred_element_type=F32
                ) + zin[1, k].astype(F32)

    @pl.when(z == 0)
    def _():
        cb[...] = fin[:, DK:]

    @pl.when(z > 0)
    def _():
        cb[...] = (
            jnp.dot(fin[:, :DK], state[...].astype(BF16), preferred_element_type=F32)
            + fin[:, DK:].astype(F32)
        ).astype(BF16)

    def sib_copy(k, sending):
        core = c if sending else 1 - c
        return rcopy(st.at[core, k], st.at[core, k], s_sib.at[k], r_sib.at[k], sibling)

    def st_copy(d, yy):
        return rcopy(cb, st.at[c, yy], s_st.at[d - 1], r_st.at[d - 1], dev(x, up(y, d, NY), z, c))

    for d in (4, 3, 5, 2, 6, 1, 7):
        st_copy(d, y).start()
    st[c, y] = cb[...]
    sib_copy(y, True).start()

    for slot in range(2):
        head = 4 * par + 2 * (1 - c) + slot
        rcopy(qbuf.at[slot, 0], q_ref.at[head], s_q.at[slot, 0], r_q.at[head], sibling).wait_recv()
        pltpu.make_async_copy(qbuf.at[slot, 0], q_ref.at[4 * par + 2 * c + slot], l_q.at[slot]).wait()
    for k in range(4):
        head = 4 * (1 - par) + k
        rcopy(qbuf.at[0, 0], q_ref.at[head], s_q.at[0, 0], r_q.at[head], sibling).wait_recv()

    def read(f, k):
        head = 4 * lax.rem(k, 2) + lax.div(k, 2)
        r = jnp.dot(q_ref[head, f], st[f, k], preferred_element_type=F32)
        r = r * lax.rsqrt(jnp.mean(r * r, axis=-1, keepdims=True) + EPS)
        lane = pl.ds(pl.multiple_of(head * DK, DK), DK)
        o_ref[f, 0, :, lane] = (r * gain_ref[:, lane]).astype(BF16)

    read(c, y)
    for d in (1, 7, 2, 6, 3, 5, 4):
        yy = down(y, d, NY)
        st_copy(d, yy).wait_recv()
        sib_copy(yy, True).start()
        read(c, yy)
    for d in (0, 1, 7, 2, 6, 3, 5, 4):
        yy = down(y, d, NY)
        sib_copy(yy, False).wait_recv()
        read(1 - c, yy)

    for slot in range(2):
        for o in range(4):
            q_out(slot, o, False)
    for slot in range(2):
        for f in range(2):
            owner, core = unit_owner(slot, f)

            @pl.when(jnp.logical_not((owner == y) & (core == c)))
            def _():
                rcopy(part.at[slot, f], got.at[0], s_g.at[slot, f], r_g.at[0], sibling).wait_send()

    for n in range(3):
        for d in range(1, NZ):
            wz_copy(n, d, z).wait_send()
        for d in range(1, NX):
            for k in range(NZ):
                wx_copy(n, d, k, x).wait_send()
    for d in range(1, NX):
        px_copy(d, x).wait_send()
    for f in range(2):
        for hf in range(2):
            for dr in range(2):
                row_copy(f, dr, hf).wait_send()
            for k in range(3):
                fwd_copy(f, k, hf, True).wait_send()
    pair.wait_send()
    for e in range(1, NZ):

        @pl.when(z + e < NZ)
        def _():
            z_copy(e).wait_send()

    for k in range(NZ - 1):

        @pl.when(k < z)
        def _():
            zs_copy(k, True).wait_send()

    for d in range(1, NY):
        st_copy(d, y).wait_send()
    for k in range(NY):
        sib_copy(k, True).wait_send()


def mix(latents, weight, beta_rows, conv_kernel, gain, step_rate, decay_rate):
    sem = pltpu.SemaphoreType.DMA
    return pl.pallas_call(
        mix_kernel,
        out_shape=jax.ShapeDtypeStruct((2, 1, 160, 1024), BF16),
        in_specs=[ANY, ANY, VM, ANY, VM, SM, SM],
        out_specs=VM,
        scratch_shapes=[
            pltpu.VMEM((2, 6, 160, 1024), BF16),
            pltpu.VMEM((3, NZ, NX, 32, 256), BF16),
            pltpu.VMEM((3, 3, 3072), F32),
            pltpu.VMEM((6, 160, 256), BF16),
            pltpu.VMEM((640, 256), BF16),
            pltpu.VMEM((640, DK), BF16),
            pltpu.VMEM((2, 2, 640, DK), F32),
            pltpu.VMEM((2, 4, 2, 160, DK), BF16),
            pltpu.VMEM((8, 2, 160, DK), BF16),
            pltpu.VMEM((2, 2, DK, 2 * DK), BF16),
            pltpu.VMEM((4, DK, 2 * DK), BF16),
            pltpu.VMEM((DK, 2 * DK), BF16),
            pltpu.VMEM((DK, 2 * DK), BF16),
            pltpu.VMEM((NX, DK, 2 * DK), BF16),
            pltpu.VMEM((2, NZ, DK, DK), BF16),
            pltpu.VMEM((DK, DK), F32),
            pltpu.VMEM((DK, DK), BF16),
            pltpu.VMEM((2, NY, DK, DK), BF16),
            sem((2, 2, 2)), sem((2, 2, 2)), sem((2, 3, 2)), sem((2, 3, 2)),
            sem((3, 7)), sem((3, 7)), sem((3, 3, 8)), sem((3, 3, 8)),
            sem((2, 2)), sem((4,)), sem((2, 4)), sem((8,)), sem((2,)), sem((9,)),
            sem(()), sem(()), sem((3,)), sem((3,)),
            sem((7,)), sem((8,)), sem((8,)), sem((8,)),
            sem((7,)), sem((7,)), sem((8,)), sem((8,)),
        ],
        compiler_params=pltpu.CompilerParams(
            collective_id=0, has_side_effects=True, vmem_limit_bytes=56 * 2**20
        ),
        name="mix",
    )(latents, weight, beta_rows, conv_kernel, gain, step_rate, decay_rate)


def body(video_latents, qkv_weight, beta_weight, conv_kernel, decay_rate, step_rate, output_gain):
    return mix(
        video_latents.reshape(2, 160, 1024), qkv_weight, beta_weight.T, conv_kernel,
        output_gain.reshape(1, 1024), step_rate, decay_rate,
    )


def solution(mesh):
    placed = (P("tm", "height", None, None), P("tm", None), P(), P(), P("tm", None), P(), P())
    return jax.shard_map(
        body, mesh=mesh, in_specs=placed, out_specs=P("tm", "height", None, None), check_vma=False
    )
```

```python
import functools

import jax
import jax.numpy as jnp
from jax import lax
from jax.experimental import pallas as pl
from jax.experimental.pallas import tpu as pltpu
from jax.sharding import PartitionSpec as P

MESH = pl.DeviceIdType.MESH
EPS = 1e-06
F32 = jnp.float32
BF16 = jnp.bfloat16
NX, NZ, NY = 4, 8, 8
TOKENS = 64 * 16 * 160
DK = 128
VM = pl.BlockSpec(memory_space=pltpu.VMEM)
SM = pl.BlockSpec(memory_space=pltpu.SMEM)
ANY = pl.BlockSpec(memory_space=pl.ANY)


def place():
    t, h = lax.axis_index("tm"), lax.axis_index("height")
    return lax.rem(t, NX), lax.div(h, 2), lax.div(t, NX), lax.rem(h, 2)


def dev(x, y, z, c):
    return (z * NX + x, y * 2 + c)


def up(i, d, n):
    return lax.rem(i + d, n)


def down(i, d, n):
    return lax.rem(i + n - d, n)


def rcopy(src, dst, ssem, rsem, to):
    return pltpu.make_async_remote_copy(
        src_ref=src, dst_ref=dst, send_sem=ssem, recv_sem=rsem, device_id=to, device_id_type=MESH
    )


def signal(barrier, to):
    pl.semaphore_signal(barrier, inc=1, device_id=to, device_id_type=MESH)


def halves(a):
    high = a.astype(BF16)
    return high, (a - high.astype(F32)).astype(BF16)


def close(a, b):
    a_high, a_low = halves(a)
    b_high, b_low = halves(b)
    both = jnp.concatenate([a_high, a_low], axis=1)
    return jnp.dot(
        both, jnp.concatenate([b_high, b_high], axis=0), preferred_element_type=F32
    ) + jnp.dot(a_high, b_low, preferred_element_type=F32)


def solve(system, ident, right):
    power = ident - 0.4 * system
    sums = jnp.concatenate([ident, right], axis=1)
    for k in range(5):
        moved = close(power, jnp.concatenate([power, sums], axis=1) if k < 4 else sums)
        sums = sums + (moved[:, DK:] if k < 4 else moved)
        power = moved[:, :DK]
    return 0.4 * sums


def mix_kernel(
    x_ref, w_ref, bw_ref, ck_hbm, gain_ref, rate_ref, decay_ref, o_ref,
    xe, wg, ck_ref, proj, kv, wt, beta, qbuf, q_ref, part, got, own, fin, px, zin, state, cb, st,
    s_row, r_row, s_fwd, r_fwd, s_wz, r_wz, s_wx, r_wx, s_g, r_g, s_q, r_q, l_q, l_in,
    s_f, r_f, s_x, r_x, s_z, r_z, s_zs, r_zs, s_st, r_st, s_sib, r_sib,
):
    x, y, z, c = place()
    par, half_y = lax.rem(y, 2), lax.div(y, 2)
    sibling = dev(x, y, z, 1 - c)
    ynext, yprev = up(y, 1, NY), down(y, 1, NY)

    loads = [pltpu.make_async_copy(x_ref.at[f], xe.at[f, 2 + c], l_in.at[f]) for f in range(2)]
    for s in range(2):
        for g in range(3):
            col = pl.multiple_of(g * 1024 + (4 * par + 2 * c + s) * 128, 128)
            block, lane = (2, s * 128) if g == 0 else (s, (g - 1) * 128)
            loads.append(
                pltpu.make_async_copy(
                    w_ref.at[:, pl.ds(col, 128)], wg.at[block, z, x, :, pl.ds(lane, 128)], l_in.at[2 + 3 * s + g]
                )
            )
    taps_in = pltpu.make_async_copy(ck_hbm, ck_ref, l_in.at[8])
    for cp in loads:
        cp.start()
    taps_in.start()

    barrier = pltpu.get_barrier_semaphore()
    for d in range(1, NZ):
        signal(barrier, dev(x, y, up(z, d, NZ), c))
    for d in range(1, NX):
        signal(barrier, dev(up(x, d, NX), y, z, c))
    for d in range(1, NY):
        for e in range(2):
            signal(barrier, dev(x, up(y, d, NY), z, e))
    signal(barrier, sibling)
    for cp in loads:
        cp.wait()
    pl.semaphore_wait(barrier, 25)

    def wz_copy(n, d, zz):
        ref = wg.at[n, zz, x]
        return rcopy(ref, ref, s_wz.at[n, d - 1], r_wz.at[n, d - 1], dev(x, y, up(z, d, NZ), c))

    def wx_copy(n, d, zz, xx):
        ref = wg.at[n, zz, xx]
        return rcopy(ref, ref, s_wx.at[n, d - 1, zz], r_wx.at[n, d - 1, zz], dev(up(x, d, NX), y, z, c))

    def wx_start(n, zz):
        for d in (2, 1, 3):
            wx_copy(n, d, zz, x).start()

    def wz_start(n):
        for d in (1, 7, 2, 6, 3, 5, 4):
            wz_copy(n, d, z).start()

    def weights_forward(n):
        for d in (1, 7, 2, 6, 3, 5, 4):
            zz = down(z, d, NZ)
            wz_copy(n, d, zz).wait_recv()
            wx_start(n, zz)

    def weights_wait(n):
        for d in range(1, NX):
            for k in range(NZ):
                wx_copy(n, d, k, down(x, d, NX)).wait_recv()

    def row_copy(f, dr, hf):
        to = dev(x, ynext, z, c) if dr == 0 else dev(x, yprev, z, c)
        cols = pl.ds(80 * hf, 80)
        return rcopy(
            xe.at[f, 2 + c, cols], xe.at[f, 4 * dr + c, cols], s_row.at[f, dr, hf], r_row.at[f, dr, hf], to
        )

    def fwd_copy(f, k, hf, sending):
        core = c if sending else 1 - c
        ref = xe.at[f, 2 * k + core, pl.ds(80 * hf, 80)]
        return rcopy(ref, ref, s_fwd.at[f, k, hf], r_fwd.at[f, k, hf], sibling)

    wz_start(0)
    wx_start(0, z)
    for f in range(2):
        for hf in range(2):
            for dr in range(2):
                row_copy(f, dr, hf).start()
        for hf in range(2):
            fwd_copy(f, 1, hf, True).start()
        if f == 0:
            wz_start(1)
            wx_start(1, z)

    def rows_forward(f):
        for hf in range(2):
            for dr in range(2):
                row_copy(f, dr, hf).wait_recv()
                fwd_copy(f, 2 * dr, hf, True).start()

    def rows_wait(f):
        for k in range(3):
            for hf in range(2):
                fwd_copy(f, k, hf, False).wait_recv()

    weights_forward(0)
    weights_forward(1)
    wz_start(2)
    rows_forward(0)
    wx_start(2, z)
    taps_in.wait()

    def gates_of(f):
        logits = lax.dot_general(
            xe[f, 1:5].reshape(640, 1024), bw_ref[...], (((1,), (1,)), ((), ())), preferred_element_type=F32
        )
        gates = jax.nn.sigmoid(logits)
        lanes = lax.broadcasted_iota(jnp.int32, (640, 8), 1)
        for s in range(2):
            picked = jnp.where(lanes == 4 * par + 2 * c + s, gates, 0.0)
            beta[f, s] = jnp.broadcast_to(jnp.sum(picked, axis=1, keepdims=True), (640, 128))

    rows_wait(0)
    gates_of(0)
    weights_wait(0)

    low = jnp.where(y == 0, 0.0, 1.0).astype(F32)
    high = jnp.where(y == NY - 1, 0.0, 1.0).astype(F32)

    def unit_owner(slot, f):
        j = 2 * c + slot
        return 2 * j + par, f

    ids = lax.broadcasted_iota(jnp.int32, (160, 128), 0)

    def project(f, n):
        proj[...] = (
            jnp.dot(
                xe[f].reshape(960, 1024), wg[n].reshape(1024, 256), preferred_element_type=F32
            )
            .astype(BF16)
            .astype(F32)
            .reshape(6, 160, 256)
        )

    def stream(part_of, head, half, o):
        col = pl.multiple_of(part_of * 1024 + head * 128, 128)
        scale = {(0, 2): low, (1, 0): low, (2, 2): high, (3, 0): high}
        sums = [None] * 3
        for a in range(3):
            row = proj[o + a, :, half * 128 : (half + 1) * 128]
            for b in range(3):
                tap = ck_ref[a, pl.ds(b, 1), pl.ds(col, 128)]
                tap = tap * scale[(o, a)] if (o, a) in scale else tap
                sums[b] = row * tap if a == 0 else sums[b] + row * tap
        total = (
            jnp.where(ids > 0, pltpu.roll(sums[0], 1, 0), 0.0)
            + sums[1]
            + jnp.where(ids < 159, pltpu.roll(sums[2], 159, 0), 0.0)
        )
        return total * jax.nn.sigmoid(total)

    def normed(s):
        return (s * lax.rsqrt(jnp.sum(s * s, axis=-1, keepdims=True) + EPS)).astype(BF16)

    def step(i, carry):
        f, slot = lax.div(i, 2), lax.rem(i, 2)

        @pl.when(i == 1)
        def _():
            weights_forward(2)
            rows_forward(1)
            weights_wait(1)

        @pl.when(i == 2)
        def _():
            rows_wait(1)
            gates_of(1)

        project(f, slot)
        head = 4 * par + 2 * c + slot
        for o in range(4):
            here = slice(o * 160, (o + 1) * 160)
            key = normed(stream(1, head, 0, o))
            kv[here, :DK] = key
            wt[here, :] = (beta[f, slot, here, :] * key.astype(F32)).astype(BF16)
            kv[here, DK:] = stream(2, head, 1, o).astype(BF16)
        unit = lax.dot_general(
            wt[...], kv[...], (((0,), (0,)), ((), ())), preferred_element_type=F32
        ).astype(BF16)
        part[slot, f] = unit
        owner, core = unit_owner(slot, f)
        here = (owner == y) & (core == c)

        @pl.when(here)
        def _():
            got[half_y] = unit

        @pl.when(jnp.logical_not(here))
        def _():
            rcopy(
                part.at[slot, f], got.at[half_y], s_g.at[slot, f], r_g.at[half_y], dev(x, owner, z, core)
            ).start()

        return carry

    lax.fori_loop(0, 4, step, 0)

    weights_wait(2)

    def query(f, carry):
        project(f, 2)
        for slot in range(2):
            for o in range(4):
                qbuf[slot, o, f] = normed(stream(0, 4 * par + 2 * c + slot, slot, o))
        return carry

    lax.fori_loop(0, 2, query, 0)

    def q_out(slot, o, send):
        head = 4 * par + 2 * c + slot
        to = {0: dev(x, yprev, z, 1), 1: dev(x, y, z, 0), 2: dev(x, y, z, 1), 3: dev(x, ynext, z, 0)}[o]

        def far():
            cp = rcopy(qbuf.at[slot, o], q_ref.at[head], s_q.at[slot, o], r_q.at[head], to)
            cp.start() if send else cp.wait_send()

        if o in (0, 3):
            far()
            return
        pl.when(c != o - 1)(far)
        if send:

            @pl.when(c == o - 1)
            def _():
                pltpu.make_async_copy(qbuf.at[slot, o], q_ref.at[head], l_q.at[slot]).start()

    for slot in range(2):
        for o in (0, 3, 1, 2):
            q_out(slot, o, True)

    step_size = rate_ref[4 * par + half_y] * (DK / TOKENS)
    retain = jnp.exp(-jnp.full((DK, DK), decay_ref[c, 4 * par + half_y], F32))
    summed = None
    for k in range(4):
        source_is_here = (k == half_y) & (lax.div(half_y, 2) == c)

        @pl.when(jnp.logical_not(source_is_here))
        def _():
            rcopy(got.at[k], got.at[k], s_g.at[0, 0], r_g.at[k], sibling).wait_recv()

        summed = got[k].astype(F32) if summed is None else summed + got[k].astype(F32)
    gram, written = summed[:, :DK], summed[:, DK:]
    diagonal = lax.broadcasted_iota(jnp.int32, (DK, DK), 0) == lax.broadcasted_iota(
        jnp.int32, (DK, DK), 1
    )
    ident = jnp.where(diagonal, 1.0, 0.0)
    maps = solve(ident + (0.5 * step_size) * (gram + gram.T), ident, step_size * written)
    own[:, :DK] = (retain * maps[:, :DK]).astype(BF16)
    own[:, DK:] = (retain * maps[:, DK:]).astype(BF16)

    def compose(latter, earlier):
        both = jnp.dot(latter[:, :DK], earlier, preferred_element_type=F32)
        return jnp.concatenate([both[:, :DK], both[:, DK:] + latter[:, DK:].astype(F32)], axis=1).astype(BF16)

    pair = rcopy(own, fin, s_f, r_f, sibling)
    pair.start()
    pair.wait_recv()
    mine, other = own[...], fin[...]
    both = compose(jnp.where(c == 0, other, mine), jnp.where(c == 0, mine, other))
    px[x] = both

    def px_copy(d, xx):
        return rcopy(px.at[xx], px.at[xx], s_x.at[d - 1], r_x.at[d - 1], dev(up(x, d, NX), y, z, c))

    for d in (2, 1, 3):
        px_copy(d, x).start()
    for d in (1, 3, 2):
        px_copy(d, down(x, d, NX)).wait_recv()
    first = compose(px[1], px[0])
    line = compose(compose(px[3], px[2]), first)
    zin[0, z] = line[:, :DK]
    zin[1, z] = line[:, DK:]

    def z_copy(e):
        return rcopy(zin.at[c, z], zin.at[c, z], s_z.at[e - 1], r_z.at[z], dev(x, y, z + e, c))

    def zs_copy(k, sending):
        core = c if sending else 1 - c
        return rcopy(zin.at[core, k], zin.at[core, k], s_zs.at[k], r_zs.at[k], sibling)

    for e in range(1, NZ):

        @pl.when(z + e < NZ)
        def _():
            z_copy(e).start()

    third = compose(px[2], first)
    current = jnp.where(c == 0, mine, both)
    before = jnp.where(x == 1, px[0], jnp.where(x == 2, first, third))
    fin[...] = jnp.where(x == 0, current, compose(current, before))

    for e in range(1, NZ):

        @pl.when(z >= e)
        def _():
            k = z - e
            rcopy(zin.at[c, k], zin.at[c, k], s_z.at[0], r_z.at[k], sibling).wait_recv()
            zs_copy(k, True).start()

    for k in range(NZ - 1):

        @pl.when(k < z)
        def _():
            zs_copy(k, False).wait_recv()
            if k == 0:
                state[...] = zin[1, 0].astype(F32)
            else:
                state[...] = jnp.dot(
                    zin[0, k], state[...].astype(BF16), preferred_element_type=F32
                ) + zin[1, k].astype(F32)

    @pl.when(z == 0)
    def _():
        cb[...] = fin[:, DK:]

    @pl.when(z > 0)
    def _():
        cb[...] = (
            jnp.dot(fin[:, :DK], state[...].astype(BF16), preferred_element_type=F32)
            + fin[:, DK:].astype(F32)
        ).astype(BF16)

    def sib_copy(k, sending):
        core = c if sending else 1 - c
        return rcopy(st.at[core, k], st.at[core, k], s_sib.at[k], r_sib.at[k], sibling)

    def st_copy(d, yy):
        return rcopy(cb, st.at[c, yy], s_st.at[d - 1], r_st.at[d - 1], dev(x, up(y, d, NY), z, c))

    for d in (4, 3, 5, 2, 6, 1, 7):
        st_copy(d, y).start()
    st[c, y] = cb[...]
    sib_copy(y, True).start()

    for slot in range(2):
        head = 4 * par + 2 * (1 - c) + slot
        rcopy(qbuf.at[slot, 0], q_ref.at[head], s_q.at[slot, 0], r_q.at[head], sibling).wait_recv()
        pltpu.make_async_copy(qbuf.at[slot, 0], q_ref.at[4 * par + 2 * c + slot], l_q.at[slot]).wait()
    for k in range(4):
        head = 4 * (1 - par) + k
        rcopy(qbuf.at[0, 0], q_ref.at[head], s_q.at[0, 0], r_q.at[head], sibling).wait_recv()

    def read(f, k):
        head = 4 * lax.rem(k, 2) + lax.div(k, 2)
        r = jnp.dot(q_ref[head, f], st[f, k], preferred_element_type=F32)
        r = r * lax.rsqrt(jnp.mean(r * r, axis=-1, keepdims=True) + EPS)
        lane = pl.ds(pl.multiple_of(head * DK, DK), DK)
        o_ref[f, 0, :, lane] = (r * gain_ref[:, lane]).astype(BF16)

    read(c, y)
    for d in (1, 7, 2, 6, 3, 5, 4):
        yy = down(y, d, NY)
        st_copy(d, yy).wait_recv()
        sib_copy(yy, True).start()
        read(c, yy)
    for d in (0, 1, 7, 2, 6, 3, 5, 4):
        yy = down(y, d, NY)
        sib_copy(yy, False).wait_recv()
        read(1 - c, yy)

    for slot in range(2):
        for o in range(4):
            q_out(slot, o, False)
    for slot in range(2):
        for f in range(2):
            owner, core = unit_owner(slot, f)

            @pl.when(jnp.logical_not((owner == y) & (core == c)))
            def _():
                rcopy(part.at[slot, f], got.at[0], s_g.at[slot, f], r_g.at[0], sibling).wait_send()

    for n in range(3):
        for d in range(1, NZ):
            wz_copy(n, d, z).wait_send()
        for d in range(1, NX):
            for k in range(NZ):
                wx_copy(n, d, k, x).wait_send()
    for d in range(1, NX):
        px_copy(d, x).wait_send()
    for f in range(2):
        for hf in range(2):
            for dr in range(2):
                row_copy(f, dr, hf).wait_send()
            for k in range(3):
                fwd_copy(f, k, hf, True).wait_send()
    pair.wait_send()
    for e in range(1, NZ):

        @pl.when(z + e < NZ)
        def _():
            z_copy(e).wait_send()

    for k in range(NZ - 1):

        @pl.when(k < z)
        def _():
            zs_copy(k, True).wait_send()

    for d in range(1, NY):
        st_copy(d, y).wait_send()
    for k in range(NY):
        sib_copy(k, True).wait_send()


def mix(latents, weight, beta_rows, conv_kernel, gain, step_rate, decay_rate):
    sem = pltpu.SemaphoreType.DMA
    return pl.pallas_call(
        mix_kernel,
        out_shape=jax.ShapeDtypeStruct((2, 1, 160, 1024), BF16),
        in_specs=[ANY, ANY, VM, ANY, VM, SM, SM],
        out_specs=VM,
        scratch_shapes=[
            pltpu.VMEM((2, 6, 160, 1024), BF16),
            pltpu.VMEM((3, NZ, NX, 32, 256), BF16),
            pltpu.VMEM((3, 3, 3072), F32),
            pltpu.VMEM((6, 160, 256), F32),
            pltpu.VMEM((640, 256), BF16),
            pltpu.VMEM((640, DK), BF16),
            pltpu.VMEM((2, 2, 640, DK), F32),
            pltpu.VMEM((2, 4, 2, 160, DK), BF16),
            pltpu.VMEM((8, 2, 160, DK), BF16),
            pltpu.VMEM((2, 2, DK, 2 * DK), BF16),
            pltpu.VMEM((4, DK, 2 * DK), BF16),
            pltpu.VMEM((DK, 2 * DK), BF16),
            pltpu.VMEM((DK, 2 * DK), BF16),
            pltpu.VMEM((NX, DK, 2 * DK), BF16),
            pltpu.VMEM((2, NZ, DK, DK), BF16),
            pltpu.VMEM((DK, DK), F32),
            pltpu.VMEM((DK, DK), BF16),
            pltpu.VMEM((2, NY, DK, DK), BF16),
            sem((2, 2, 2)), sem((2, 2, 2)), sem((2, 3, 2)), sem((2, 3, 2)),
            sem((3, 7)), sem((3, 7)), sem((3, 3, 8)), sem((3, 3, 8)),
            sem((2, 2)), sem((4,)), sem((2, 4)), sem((8,)), sem((2,)), sem((9,)),
            sem(()), sem(()), sem((3,)), sem((3,)),
            sem((7,)), sem((8,)), sem((8,)), sem((8,)),
            sem((7,)), sem((7,)), sem((8,)), sem((8,)),
        ],
        compiler_params=pltpu.CompilerParams(
            collective_id=0, has_side_effects=True, vmem_limit_bytes=56 * 2**20
        ),
        name="mix",
    )(latents, weight, beta_rows, conv_kernel, gain, step_rate, decay_rate)


def body(video_latents, qkv_weight, beta_weight, conv_kernel, decay_rate, step_rate, output_gain):
    return mix(
        video_latents.reshape(2, 160, 1024), qkv_weight, beta_weight.T, conv_kernel,
        output_gain.reshape(1, 1024), step_rate, decay_rate,
    )


def solution(mesh):
    placed = (P("tm", "height", None, None), P("tm", None), P(), P(), P("tm", None), P(), P())
    return jax.shard_map(
        body, mesh=mesh, in_specs=placed, out_specs=P("tm", "height", None, None), check_vma=False
    )
```
